256 devices in a mesh: member: 8 (over y, core), rows: 32 (over z, x).
Axes of the slice: x: 4, y: 4, z: 8, core: 2. Of those that a mesh axis runs over, the one named last changes fastest.
Arguments:
- processed_latent_nodes: bfloat16 [8, 16384, 1024], P('member', 'rows'), may hold values from -6 to 6
- grid_embed: bfloat16 [49152, 1024], P('rows'), may hold values from -6 to 6
- dispatch_node_lookup: int32 [1024, 128], P('rows'), may hold values from 0 to 511
- send_count: int32 [1024], P('rows'), may hold values from 1 to 128, as said below
- edge_slot: int32 [3, 49152], P(None, 'rows'), may hold values from 0 to 4095, as said below
- row_points: int32 [32], P('rows'), may hold values from 384 to 1536, as said below
- w_src: bfloat16 [1024, 1024], replicated, may hold values from -0.1875 to 0.1875
- w_dst: bfloat16 [1024, 1024], replicated, may hold values from -0.1875 to 0.1875
- gain_node: float32 [1024], replicated, may hold values from 0.1 to 1.9
- w_node: bfloat16 [1024, 1024], replicated, may hold values from -0.1875 to 0.1875
- w_out: bfloat16 [100, 1024], replicated, may hold values from -0.1875 to 0.1875
- targets: float32 [100, 49152], P(None, 'rows'), may hold values from -6 to 6
- channel_weight: float32 [100], replicated, may hold values from 0.25 to 4
Outputs:
- realization_fields_out: bfloat16 [8, 100, 49152], P('member', None, 'rows')
- score_slope_array: float32 [8, 100, 49152], P('member', None, 'rows')
The draws below stay inside these ranges and needn't reach their ends.
Inputs may be any that keep to these rules, and one draw needn't show every extreme that they name: `send_count`: slots sent from one shard to one owner; every shard sends all 128 to some owner and one slot to another. `edge_slot`: each edge reads a live slot: c is below send_count of sender s to the point's owner. `row_points`: some slab is full and some holds a quarter of its slots.
All inputs are finite; a program needn't handle non-finite values.
Results may differ from the reference program's by a relative error of at most 0.006.
Values may be sent and summed in bfloat16 or wider, within the bound.
A program may use at most 128 MiB of HBM per device.

```python
import math
import jax
import jax.numpy as jnp
from jax import lax

D = 1024
H = 1024
C = 100
K = 3
CAP = 128
MN_DEV = 512
G_DEV = 1536
MEMBERS = 8
MESH = 16384
GRID = 49152
N_ROWS = 32


def count_table(key):
    key = jax.random.fold_in(key, 101)
    first, second, third = jax.random.split(key, 3)
    counts = jax.random.randint(first, (N_ROWS, N_ROWS), 1, CAP + 1)
    full_at = jax.random.randint(second, (N_ROWS, 1), 0, N_ROWS)
    one_at = (full_at + jax.random.randint(third, (N_ROWS, 1), 1, N_ROWS)) % N_ROWS
    columns = jnp.arange(N_ROWS, dtype=jnp.int32)[None, :]
    counts = jnp.where(columns == one_at, 1, counts)
    counts = jnp.where(columns == full_at, CAP, counts)
    return counts.astype(jnp.int32)


def draw_send_count(key, part):
    counts = count_table(key)
    return counts.reshape(N_ROWS * N_ROWS)


def draw_edge_slot(key, part):
    counts = count_table(key)
    key = jax.random.fold_in(key, 11)
    first, second = jax.random.split(key)
    owner_of = (jnp.arange(GRID, dtype=jnp.int32) // G_DEV)[None, :]
    sender = jax.random.randint(first, (K, GRID), 0, N_ROWS)
    limit = counts[sender, owner_of]
    column = jax.random.randint(second, (K, GRID), 0, limit)
    return (sender * CAP + column).astype(jnp.int32)


def draw_row_points(key, part):
    key = jax.random.fold_in(key, 13)
    first, second, third = jax.random.split(key, 3)
    points = jax.random.randint(first, (N_ROWS,), G_DEV // 4, G_DEV + 1)
    full_at = jax.random.randint(second, (), 0, N_ROWS)
    least_at = (full_at + jax.random.randint(third, (), 1, N_ROWS)) % N_ROWS
    places = jnp.arange(N_ROWS, dtype=jnp.int32)
    points = jnp.where(places == least_at, G_DEV // 4, points)
    points = jnp.where(places == full_at, G_DEV, points)
    return points.astype(jnp.int32)


def with_ends(values, rng, low, largest):
    spot = [jax.random.randint(jax.random.fold_in(rng, axis), (), 0, length) for axis, length in enumerate(values.shape)]
    main_axis = values.shape.index(max(values.shape))
    beside = spot[:main_axis] + [(spot[main_axis] + 1) % values.shape[main_axis]] + spot[main_axis + 1:]
    return values.at[tuple(spot)].set(low).at[tuple(beside)].set(largest)


def block_levels(rng, dims, cuts, smallest, top_value):
    gain, own = 1.0, jax.random.fold_in(rng, 6)
    for position, blocks in cuts:
        heights = jnp.exp(jax.random.uniform(jax.random.fold_in(own, position), (blocks,), jnp.float32, smallest / len(cuts), top_value / len(cuts)))
        gain = gain * jnp.repeat(heights, dims[position] // blocks).reshape([-1 if axis == position else 1 for axis in range(len(dims))])
    return gain


def noise(own_key, dims, spread, most, pieces=(), kind=jnp.bfloat16):
    drawn = jax.random.normal(own_key, dims, jnp.float32) * spread
    if len(pieces) > 0:
        drawn = block_levels(own_key, dims, pieces, -0.22, 0.18) * drawn
    return jnp.clip(drawn, min=-most, max=most).astype(kind)


def setup_inputs(seed: int = 0) -> dict:
    splits = jax.random.split(jax.random.key(seed), 14)
    return {
        "processed_latent_nodes": noise(splits[0], (MEMBERS, MESH, D), 1.0, 6.0, ((0, 8), (1, 32))),
        "grid_embed": noise(splits[1], (GRID, D), 1.0, 6.0, ((0, 32),)),
        "dispatch_node_lookup": with_ends(jax.random.randint(splits[2], (N_ROWS * N_ROWS, CAP), 0, MN_DEV), jax.random.fold_in(splits[2], 1), 0, MN_DEV - 1).astype(jnp.int32),
        "send_count": draw_send_count(jax.random.fold_in(splits[13], 71), 0),
        "edge_slot": draw_edge_slot(jax.random.fold_in(splits[13], 71), 0),
        "row_points": draw_row_points(jax.random.fold_in(splits[13], 71), 0),
        "w_src": noise(splits[6], (D, H), D ** -0.5, 0.1875),
        "w_dst": noise(splits[7], (D, H), D ** -0.5, 0.1875),
        "gain_node": jnp.clip(1.0 + 0.18 * jax.random.normal(splits[8], (H,), jnp.float32), 0.1, 1.9),
        "w_node": noise(splits[9], (H, H), H ** -0.5, 0.1875),
        "w_out": noise(splits[10], (C, H), H ** -0.5, 0.1875),
        "targets": noise(splits[11], (C, GRID), 1.0, 6.0, ((1, 32),), jnp.float32),
        "channel_weight": jnp.clip(jnp.exp(jax.random.uniform(splits[12], (C,), jnp.float32, math.log(0.25), math.log(4.0))), 0.25, 4.0),
    }


SOFT_SCALE = 0.5
EPSILON = 1e-05

def soft_slope(grid_point_entries):
    return grid_point_entries / jnp.sqrt(grid_point_entries * grid_point_entries + SOFT_SCALE * SOFT_SCALE)

def reference(processed_latent_nodes, grid_embed, dispatch_node_lookup, send_count, edge_slot, row_points, w_src, w_dst, gain_node, w_node, w_out, targets, channel_weight):
    points = jnp.arange(GRID, dtype=jnp.int32)
    owner_of = (points // G_DEV)[None, :]
    sender = edge_slot // CAP
    column = edge_slot % CAP
    sender_owner = sender * N_ROWS + owner_of
    local_row = dispatch_node_lookup[sender_owner, column]
    live_slot = column < send_count[sender_owner]
    mesh_row = sender * MN_DEV + local_row
    exists_indicator = points % G_DEV < row_points[points // G_DEV]
    grid_side = jnp.dot(grid_embed, w_dst, preferred_element_type=jnp.float32)

    def expand_lone_realization(realization_lines):
        projected = jnp.dot(realization_lines, w_src, preferred_element_type=jnp.float32).astype(jnp.bfloat16)
        summed = jnp.zeros((GRID, H), jnp.float32)
        for which in range(K):
            edge_in = jnp.where(live_slot[which][:, None], projected[mesh_row[which]].astype(jnp.float32), 0.0)
            summed = summed + jax.nn.silu(edge_in + grid_side)
        scale = lax.rsqrt(lax.optimization_barrier(jnp.mean(summed * summed, axis=-1, keepdims=True)) + EPSILON)
        normed = (summed * scale * gain_node[None, :]).astype(jnp.bfloat16)
        hidden = jax.nn.silu(jnp.dot(normed, w_node, preferred_element_type=jnp.float32)).astype(jnp.bfloat16)
        expanded_fields = lax.dot_general(w_out, hidden, (((1,), (1,)), ((), ())), preferred_element_type=jnp.float32)
        return jnp.where(exists_indicator[None, :], expanded_fields, 0.0).astype(jnp.bfloat16)
    realization_fields_out = lax.map(expand_lone_realization, processed_latent_nodes)
    grid_point_entries = realization_fields_out.astype(jnp.float32)

    def member_gradient(shard_grid_entries):
        pair_sum = lax.optimization_barrier(jnp.sum(soft_slope(shard_grid_entries[None] - grid_point_entries), axis=0))
        slope_sum = soft_slope(shard_grid_entries - targets) - pair_sum / (MEMBERS - 1)
        return jnp.where(exists_indicator[None, :], channel_weight[:, None] * slope_sum, 0.0)
    score_slope_array = lax.map(member_gradient, grid_point_entries)
    return (realization_fields_out, score_slope_array)
```

```python
import functools

import jax
import jax.numpy as jnp
from jax import lax
from jax.experimental import pallas as pl
from jax.experimental.pallas import tpu as pltpu
from jax.sharding import PartitionSpec as P

SOFT_SCALE = 0.5
EPSILON = 1e-05
MESH = pl.DeviceIdType.MESH

NZ, NX, NY = 8, 4, 4
ROWS = NZ * NX
MEMBERS = 8
CAP = 128
NODES = 512
D = 1024
W = 512
G = 1536
C = 100
CP = 112
K = 3
PB = 256
MIB = 1 << 20


def row_id(z, x):
    return lax.rem(z, NZ) * NX + lax.rem(x, NX)


def table_kernel(
    latent, w_src, look, embed_hbm, wdst_hbm, tab, gs_out,
    T, stage, fwd_p, fwd_m, L, LC, embed, wdst, gs,
    lk_s, lk_r, z_s, z_r, x_s, x_r, loc, pre,
):
    me = lax.axis_index("rows")
    z = me // NX
    x = lax.rem(me, NX)

    barrier = pltpu.get_barrier_semaphore()
    peers = [row_id(z + k, x) for k in range(1, NZ)]
    peers += [row_id(z, x + 1), row_id(z, x + 3)]
    for peer in peers:
        pl.semaphore_signal(barrier, inc=1, device_id={"rows": peer}, device_id_type=MESH)

    load_embed = pltpu.make_async_copy(embed_hbm, embed, pre.at[0])
    load_wdst = pltpu.make_async_copy(wdst_hbm, wdst, pre.at[1])
    load_embed.start()
    load_wdst.start()

    def project(h):
        @pl.loop(0, NODES // 128)
        def _(i):
            rows = pl.ds(pl.multiple_of(i * 128, 128), 128)
            T[h, z, rows, :] = jnp.dot(
                latent[rows, :], w_src[:, h * W:(h + 1) * W],
                preferred_element_type=jnp.float32,
            ).astype(jnp.bfloat16)

    def remote(src, dst, ss, rs, to):
        return pltpu.make_async_remote_copy(
            src_ref=src, dst_ref=dst, send_sem=ss, recv_sem=rs,
            device_id={"rows": to}, device_id_type=MESH,
        )

    def z_copy(direction, d, h):
        if direction == 0:
            shard, to = lax.rem(z + NZ - (d - 1), NZ), row_id(z + 1, x)
        else:
            shard, to = lax.rem(z + (d - 1), NZ), row_id(z + NZ - 1, x)
        i = (direction * 4 + d - 1) * 2 + h
        return remote(T.at[h, shard], T.at[h, shard], z_s.at[i], z_r.at[i], to)

    def z_arrival(direction, d, h):
        if direction == 0:
            shard = lax.rem(z + NZ - d, NZ)
        else:
            shard = lax.rem(z + d, NZ)
        i = (direction * 4 + d - 1) * 2 + h
        return remote(T.at[h, shard], T.at[h, shard], z_s.at[i], z_r.at[i], row_id(z + 1, x))

    def lk_copy(k):
        to_z = lax.rem(z + k, NZ)
        return remote(look.at[to_z], L.at[z], lk_s.at[k], lk_r.at[z], row_id(to_z, x))

    def lk_arrival(shard):
        return remote(look.at[shard], L.at[shard], lk_s.at[0], lk_r.at[shard], row_id(z + 1, x))

    def x_copies(h, shard, item):
        right, left = row_id(z, x + 1), row_id(z, x + 3)
        own = shard * NX + x
        base = item * 6
        to_right = stage.at[h, shard, lax.rem(x + 1, NX)]
        to_left = stage.at[h, shard, lax.rem(x + 3, NX)]
        far = stage.at[h, shard, lax.rem(x + 2, NX)]
        return [
            remote(far.at[pl.ds(0, 64)], fwd_p.at[h, shard], x_s.at[base + 2], x_r.at[base + 2], right),
            remote(far.at[pl.ds(64, 64)], fwd_m.at[h, shard], x_s.at[base + 3], x_r.at[base + 3], left),
            remote(to_right, tab.at[h, own], x_s.at[base], x_r.at[base], right),
            remote(to_left, tab.at[h, own], x_s.at[base + 1], x_r.at[base + 1], left),
        ]

    def x_forwards(h, shard, item):
        right, left = row_id(z, x + 1), row_id(z, x + 3)
        base = item * 6
        return [
            remote(
                fwd_p.at[h, shard],
                tab.at[h, shard * NX + lax.rem(x + 3, NX), pl.ds(0, 64)],
                x_s.at[base + 4], x_r.at[base + 4], right,
            ),
            remote(
                fwd_m.at[h, shard],
                tab.at[h, shard * NX + lax.rem(x + 1, NX), pl.ds(64, 64)],
                x_s.at[base + 5], x_r.at[base + 5], left,
            ),
        ]

    def x_arrivals(h, shard, item):
        base = item * 6
        to = row_id(z, x + 1)
        far = shard * NX + lax.rem(x + 2, NX)
        spots = [
            tab.at[h, shard * NX + lax.rem(x + 3, NX)],
            tab.at[h, shard * NX + lax.rem(x + 1, NX)],
            fwd_p.at[h, shard],
            fwd_m.at[h, shard],
            tab.at[h, far, pl.ds(0, 64)],
            tab.at[h, far, pl.ds(64, 64)],
        ]
        return [remote(s, s, x_s.at[base + i], x_r.at[base + i], to) for i, s in enumerate(spots)]

    def local_copy(h, shard, item):
        return pltpu.make_async_copy(stage.at[h, shard, x], tab.at[h, shard * NX + x], loc.at[item])

    def columns(shard):
        for r in range(NX):
            line = jnp.broadcast_to(L[shard, r:r + 1, :], (128, 128))
            LC[shard, r] = jnp.transpose(line)

    def select(h, shard):
        @pl.loop(0, NX)
        def _(r):
            col = LC[shard, r]
            lane = lax.broadcasted_iota(jnp.int32, (CAP, 128), 1)
            hot = jnp.concatenate(
                [jnp.where(col == lane + 128 * t, 1.0, 0.0) for t in range(NODES // 128)], axis=1
            ).astype(jnp.bfloat16)
            stage[h, shard, r] = jnp.dot(
                hot, T[h, shard], preferred_element_type=jnp.float32
            ).astype(jnp.bfloat16)

    def launch(h, shard, item):
        select(h, shard)
        for copy in x_copies(h, shard, item):
            copy.start()
        local_copy(h, shard, item).start()

    def forward(h, shard, item):
        arrived = x_arrivals(h, shard, item)
        copies = x_forwards(h, shard, item)
        arrived[2].wait_recv()
        copies[0].start()
        arrived[3].wait_recv()
        copies[1].start()

    project(0)
    pl.semaphore_wait(barrier, len(peers))
    z_copy(0, 1, 0).start()
    z_copy(1, 1, 0).start()
    for k in range(1, NZ):
        lk_copy(k).start()
    project(1)
    z_copy(0, 1, 1).start()
    z_copy(1, 1, 1).start()

    L[z] = look[z]
    columns(z)
    items = []
    for h in range(2):
        items.append((h, z, len(items)))
        launch(*items[-1])

    load_embed.wait()
    load_wdst.wait()

    def grid_side(part):
        @pl.loop(part * 3, part * 3 + 3)
        def _(i):
            rows = pl.ds(pl.multiple_of(i * 128, 128), 128)
            for j in range(4):
                value = jnp.dot(
                    embed[rows, :], wdst[:, j * 256:(j + 1) * 256], preferred_element_type=jnp.float32
                )
                for r in range(16):
                    for t in range(2):
                        gs[pl.ds((i * 128 + r * 8) * 8 + j * 2 + t, 8, stride=8), :] = 0.5 * value[
                            r * 8:(r + 1) * 8, t * 128:(t + 1) * 128
                        ]

    grid_side(0)
    grid_side(1)
    served = 0
    pending = list(items)
    for d in range(1, 4):
        below = lax.rem(z + NZ - d, NZ)
        above = lax.rem(z + d, NZ)
        for h in range(2):
            z_arrival(0, d, h).wait_recv()
            if d < 3 or h == 0:
                z_copy(0, d + 1, h).start()
            z_arrival(1, d, h).wait_recv()
            if d < 3 or h == 1:
                z_copy(1, d + 1, h).start()
            if h == 0:
                for shard in (below, above):
                    lk_arrival(shard).wait_recv()
                    columns(shard)
            for item in pending:
                forward(*item)
            pending = []
            for shard in (below, above):
                items.append((h, shard, len(items)))
                pending.append(items[-1])
                launch(*items[-1])
        if d == 1:
            grid_side(2)
            grid_side(3)
            save_gs = pltpu.make_async_copy(gs, gs_out, pre.at[2])
            save_gs.start()
    last = lax.rem(z + 4, NZ)
    lk_arrival(last).wait_recv()
    columns(last)
    for h in range(2):
        z_arrival(h, 4, h).wait_recv()
        for item in pending:
            forward(*item)
        items.append((h, last, len(items)))
        pending = [items[-1]]
        launch(*items[-1])
    for item in pending:
        forward(*item)

    for item in items:
        arrived = x_arrivals(*item)
        for i in (0, 1, 4, 5):
            arrived[i].wait_recv()
        for copy in x_copies(*item) + x_forwards(*item):
            copy.wait_send()
        local_copy(*item).wait()
    for d in range(1, 5):
        for h in range(2):
            for direction in range(2):
                if d < 4 or h == direction:
                    z_copy(direction, d, h).wait_send()
    for k in range(1, NZ):
        lk_copy(k).wait_send()
    save_gs.wait()


def table_call(latent, w_src, look, embed, w_dst):
    n_items = 2 * NZ
    vm = pl.BlockSpec(memory_space=pltpu.VMEM)
    hbm = pl.BlockSpec(memory_space=pl.ANY)
    dma = pltpu.SemaphoreType.DMA
    return pl.pallas_call(
        table_kernel,
        out_shape=(
            jax.ShapeDtypeStruct((2, ROWS, CAP, W), jnp.bfloat16),
            jax.ShapeDtypeStruct((G * 8, 128), jnp.float32),
        ),
        in_specs=[vm, vm, vm, hbm, hbm],
        out_specs=(hbm, hbm),
        scratch_shapes=[
            pltpu.VMEM((2, NZ, NODES, W), jnp.bfloat16),
            pltpu.VMEM((2, NZ, NX, CAP, W), jnp.bfloat16),
            pltpu.VMEM((2, NZ, 64, W), jnp.bfloat16),
            pltpu.VMEM((2, NZ, 64, W), jnp.bfloat16),
            pltpu.VMEM((NZ, NX, CAP), jnp.int32),
            pltpu.VMEM((NZ, NX, CAP, 128), jnp.int32),
            pltpu.VMEM((G, D), jnp.bfloat16),
            pltpu.VMEM((D, D), jnp.bfloat16),
            pltpu.VMEM((G * 8, 128), jnp.float32),
            dma((NZ,)), dma((NZ,)),
            dma((16,)), dma((16,)),
            dma((n_items * 6,)), dma((n_items * 6,)),
            dma((n_items,)), dma((3,)),
        ],
        compiler_params=pltpu.CompilerParams(
            collective_id=0, has_side_effects=True, vmem_limit_bytes=56 * MIB
        ),
        cost_estimate=pl.CostEstimate(flops=14 * 10**9, bytes_accessed=30 * MIB, transcendentals=0),
        name="table",
    )(latent, w_src, look, embed, w_dst)


def decode_kernel(edge, rp, tab, gs, w_node, w_out, gain, out, F, S):
    @pl.loop(0, ROWS)
    def _(s):
        for r in range(CAP // 16):
            for h in range(2):
                value = tab[h, s, r * 16:(r + 1) * 16, :].astype(jnp.float32) * 0.5
                for u in range(2):
                    for j in range(4):
                        start = (s * CAP + r * 16 + u * 8) * 8 + h * 4 + j
                        F[pl.ds(start, 8, stride=8), :] = value[
                            u * 8:(u + 1) * 8, j * 128:(j + 1) * 128
                        ]

    gain_row = gain[...]

    @pl.loop(0, G // PB)
    def _(b):
        first = b * PB

        @pl.loop(0, PB // 8)
        def _(q):
            for u in range(8):
                p = first + q * 8 + u
                g = gs[pl.ds(pl.multiple_of(p * 8, 8), 8), :]
                total = jnp.zeros((8, 128), jnp.float32)
                for k in range(K):
                    row = pl.multiple_of(edge[k, p] * 8, 8)
                    half = F[pl.ds(row, 8), :] + g
                    total = total + (half + half * jnp.tanh(half))
                S[pl.ds(q * 64 + u, 8, stride=8), :] = total

        cube = S[...].reshape(PB // 8, 8, 8, 128)
        summed = jnp.concatenate([cube[:, j].reshape(PB, 128) for j in range(8)], axis=1)
        scale = lax.rsqrt(jnp.mean(summed * summed, axis=-1, keepdims=True) + EPSILON)
        normed = (summed * scale * gain_row).astype(jnp.bfloat16)
        half = 0.5 * jnp.dot(normed, w_node[...], preferred_element_type=jnp.float32)
        hidden = (half + half * jnp.tanh(half)).astype(jnp.bfloat16)
        fields = lax.dot_general(
            w_out[...], hidden, (((1,), (1,)), ((), ())), preferred_element_type=jnp.float32
        )
        point = lax.broadcasted_iota(jnp.int32, (C, PB), 1) + first
        lanes = pl.ds(pl.multiple_of(lax.rem(b, 3) * PB, 128), PB)
        out[b // 3, 0:C, lanes] = jnp.where(point < rp[0], fields, 0.0).astype(jnp.bfloat16)
        out[b // 3, C:CP, lanes] = jnp.zeros((CP - C, PB), jnp.bfloat16)


def decode_call(edge, rp, tab, gs, w_node, w_out, gain):
    vm = pl.BlockSpec(memory_space=pltpu.VMEM)
    sm = pl.BlockSpec(memory_space=pltpu.SMEM)
    return pl.pallas_call(
        decode_kernel,
        out_shape=jax.ShapeDtypeStruct((2, CP, G // 2), jnp.bfloat16),
        in_specs=[sm, sm, vm, vm, vm, vm, vm],
        out_specs=vm,
        scratch_shapes=[
            pltpu.VMEM((ROWS * CAP * 8, 128), jnp.float32),
            pltpu.VMEM((PB * 8, 128), jnp.float32),
        ],
        compiler_params=pltpu.CompilerParams(vmem_limit_bytes=56 * MIB),
        name="decode",
    )(edge, rp, tab, gs, w_node, w_out, gain)


def score_kernel(rp, mine, targets, weight, fields_out, score_out, X, send, recv):
    m = lax.axis_index("member")
    y = m // 2
    c = lax.rem(m, 2)

    def chip(k):
        return lax.rem(y + k, NY) * 2

    up, down, far, partner = chip(1) + c, chip(3) + c, chip(2) + c, chip(0) + 1 - c
    barrier = pltpu.get_barrier_semaphore()
    for peer in (up, down, partner):
        pl.semaphore_signal(barrier, inc=1, device_id={"member": peer}, device_id_type=MESH)
    pl.semaphore_wait(barrier, 3)

    def remote(src, dst, i, to):
        return pltpu.make_async_remote_copy(
            src_ref=src, dst_ref=dst, send_sem=send.at[i], recv_sem=recv.at[i],
            device_id={"member": to}, device_id_type=MESH,
        )

    own = [
        remote(mine.at[0], X.at[m, 0], 0, up),
        remote(mine.at[1], X.at[m, 1], 1, down),
        remote(mine.at[1], X.at[m, 1], 2, up),
        remote(mine.at[0], X.at[m, 0], 3, down),
        remote(mine, X.at[m], 4, partner),
    ]
    landed = [
        remote(X.at[down, 0], X.at[down, 0], 0, up),
        remote(X.at[up, 1], X.at[up, 1], 1, up),
        remote(X.at[down, 1], X.at[down, 1], 2, up),
        remote(X.at[up, 0], X.at[up, 0], 3, up),
        remote(X.at[partner], X.at[partner], 4, up),
    ]
    passed = [
        remote(X.at[down, 0], X.at[down, 0], 5, up),
        remote(X.at[up, 1], X.at[up, 1], 6, down),
    ]
    passed_landed = [
        remote(X.at[far, 0], X.at[far, 0], 5, up),
        remote(X.at[far, 1], X.at[far, 1], 6, up),
    ]
    o = 1 - 2 * c
    across = [
        remote(X.at[down], X.at[down], 7, partner),
        remote(X.at[up], X.at[up], 8, partner),
        remote(X.at[far], X.at[far], 9, partner),
    ]
    across_landed = [
        remote(X.at[down + o], X.at[down + o], 7, up),
        remote(X.at[up + o], X.at[up + o], 8, up),
        remote(X.at[far + o], X.at[far + o], 9, up),
    ]
    for copy in own:
        copy.start()
    X[m] = mine[...]
    landed[0].wait_recv()
    passed[0].start()
    landed[1].wait_recv()
    passed[1].start()
    landed[2].wait_recv()
    across[0].start()
    landed[3].wait_recv()
    across[1].start()
    passed_landed[0].wait_recv()
    passed_landed[1].wait_recv()
    across[2].start()
    landed[4].wait_recv()
    for copy in across_landed:
        copy.wait_recv()

    def slope(v):
        return v * lax.rsqrt(v * v + SOFT_SCALE * SOFT_SCALE)

    scale = weight[...]

    @pl.loop(0, G // 128)
    def _(t):
        half = t // 6
        lanes = pl.ds(pl.multiple_of(lax.rem(t, 6) * 128, 128), 128)
        whole = pl.ds(pl.multiple_of(t * 128, 128), 128)
        raw = mine[half, 0:C, lanes]
        here = raw.astype(jnp.float32)
        pair = jnp.zeros((C, 128), jnp.float32)
        for j in range(MEMBERS):
            pair = pair + slope(here - X[j, half, 0:C, lanes].astype(jnp.float32))
        total = slope(here - targets[:, whole]) - pair * (1.0 / (MEMBERS - 1))
        point = lax.broadcasted_iota(jnp.int32, (C, 128), 1) + t * 128
        fields_out[:, whole] = raw
        score_out[:, whole] = jnp.where(point < rp[0], scale * total, 0.0)

    for copy in own + passed + across:
        copy.wait_send()


def score_call(rp, mine, targets, weight):
    vm = pl.BlockSpec(memory_space=pltpu.VMEM)
    sm = pl.BlockSpec(memory_space=pltpu.SMEM)
    return pl.pallas_call(
        score_kernel,
        out_shape=(
            jax.ShapeDtypeStruct((C, G), jnp.bfloat16),
            jax.ShapeDtypeStruct((C, G), jnp.float32),
        ),
        in_specs=[sm, vm, vm, vm],
        out_specs=(vm, vm),
        scratch_shapes=[
            pltpu.VMEM((MEMBERS, 2, CP, G // 2), jnp.bfloat16),
            pltpu.SemaphoreType.DMA((10,)),
            pltpu.SemaphoreType.DMA((10,)),
        ],
        compiler_params=pltpu.CompilerParams(
            collective_id=1, has_side_effects=True, vmem_limit_bytes=32 * MIB
        ),
        name="score",
    )(rp, mine, targets, weight)


def local(
    processed_latent_nodes, grid_embed, dispatch_node_lookup, send_count, edge_slot, row_points,
    w_src, w_dst, gain_node, w_node, w_out, targets, channel_weight,
):
    del send_count
    look = dispatch_node_lookup.reshape(NZ, NX, CAP)
    tab, gs = table_call(processed_latent_nodes[0], w_src, look, grid_embed, w_dst)
    mine = decode_call(edge_slot, row_points, tab, gs, w_node, w_out, gain_node[None, :])
    fields, score = score_call(row_points, mine, targets, channel_weight[:, None])
    return fields[None], score[None]


def solution(mesh):
    placed = (
        P("member", "rows", None),
        P("rows", None),
        P("rows", None),
        P("rows"),
        P(None, "rows"),
        P("rows"),
        P(),
        P(),
        P(),
        P(),
        P(),
        P(None, "rows"),
        P(),
    )
    return jax.shard_map(
        local,
        mesh=mesh,
        in_specs=placed,
        out_specs=(P("member", None, "rows"), P("member", None, "rows")),
        check_vma=False,
    )
```

```python
import functools

import jax
import jax.numpy as jnp
from jax import lax
from jax.experimental import pallas as pl
from jax.experimental.pallas import tpu as pltpu
from jax.sharding import PartitionSpec as P

SOFT_SCALE = 0.5
EPSILON = 1e-05
MESH = pl.DeviceIdType.MESH

NZ, NX, NY = 8, 4, 4
ROWS = NZ * NX
MEMBERS = 8
CAP = 128
NODES = 512
D = 1024
W = 512
G = 1536
C = 100
CP = 112
K = 3
PB = 256
NB = G // PB
SLOTS = 8
MIB = 1 << 20
VMEM_LIMIT = 63 * MIB


def row_id(z, x):
    return lax.rem(z, NZ) * NX + lax.rem(x, NX)


def decoder_kernel(
    edge, rp, latent, w_src, look, gain, weight,
    embed_hbm, wdst_hbm, wnode_hbm, wout_hbm, targets_hbm,
    fields_out, score_out,
    T, stage, landing, fwd_p, fwd_m, L, LC, F, gs, S, X,
    embed, wdst, w_node, w_out, targets,
    lk_s, lk_r, z_s, z_r, x_s, x_r, m_s, m_r, pre,
):
    me = lax.axis_index("rows")
    z = me // NX
    x = lax.rem(me, NX)
    m = lax.axis_index("member")
    y = m // 2
    c = lax.rem(m, 2)
    right, left = row_id(z, x + 1), row_id(z, x + 3)
    north, south = row_id(z + 1, x), row_id(z + NZ - 1, x)

    flat = F.reshape(ROWS * CAP * 8, 128)

    def chip(k):
        return lax.rem(y + k, NY) * 2

    up, down, far, partner = chip(1) + c, chip(3) + c, chip(2) + c, chip(0) + 1 - c
    other = 1 - 2 * c

    barrier = pltpu.get_barrier_semaphore()
    peers = [{"rows": row_id(z + k, x)} for k in range(1, NZ)]
    peers += [{"rows": right}, {"rows": left}]
    peers += [{"member": up}, {"member": down}, {"member": partner}]
    for peer in peers:
        pl.semaphore_signal(barrier, inc=1, device_id=peer, device_id_type=MESH)

    loads = [
        pltpu.make_async_copy(a, b, pre.at[i])
        for i, (a, b) in enumerate([
            (embed_hbm, embed), (wdst_hbm, wdst), (wnode_hbm, w_node), (wout_hbm, w_out),
            (targets_hbm, targets),
        ])
    ]
    for load in loads:
        load.start()

    def remote(src, dst, ss, rs, **to):
        return pltpu.make_async_remote_copy(
            src_ref=src, dst_ref=dst, send_sem=ss, recv_sem=rs,
            device_id=to, device_id_type=MESH,
        )

    def project(h):
        @pl.loop(0, NODES // 128)
        def _(i):
            rows = pl.ds(pl.multiple_of(i * 128, 128), 128)
            T[h, z, rows, :] = jnp.dot(
                latent[rows, :], w_src[:, h * W:(h + 1) * W],
                preferred_element_type=jnp.float32,
            ).astype(jnp.bfloat16)

    def z_copy(direction, d, h, arriving=False):
        back = d if arriving else d - 1
        shard = lax.rem(z + NZ - back, NZ) if direction == 0 else lax.rem(z + back, NZ)
        i = (direction * 4 + d - 1) * 2 + h
        return remote(
            T.at[h, shard], T.at[h, shard], z_s.at[i], z_r.at[i],
            rows=north if direction == 0 else south,
        )

    def lk_copy(k):
        to_z = lax.rem(z + k, NZ)
        return remote(look.at[to_z], L.at[z], lk_s.at[k], lk_r.at[z], rows=row_id(to_z, x))

    def lk_arrival(shard):
        return remote(look.at[shard], L.at[shard], lk_s.at[0], lk_r.at[shard], rows=north)

    def x_copy(i, item):
        n = item[2]
        slot = n % SLOTS
        src, dst, to = [
            (stage.at[slot, 0], landing.at[n, 2], right),
            (stage.at[slot, 2], landing.at[n, 0], left),
            (stage.at[slot, 1, pl.ds(0, 64)], fwd_p.at[n], right),
            (stage.at[slot, 1, pl.ds(64, 64)], fwd_m.at[n], left),
            (fwd_p.at[n], landing.at[n, 1, pl.ds(0, 64)], right),
            (fwd_m.at[n], landing.at[n, 1, pl.ds(64, 64)], left),
        ][i]
        return remote(src, dst, x_s.at[n * 6 + i], x_r.at[n * 6 + i], rows=to)

    def columns(shard, place):
        for r in range(NX):
            line = jnp.broadcast_to(L[shard, pl.ds(lax.rem(x + r, NX), 1), :], (128, 128))
            LC[place, r] = jnp.transpose(line)

    def to_rows(value, h, first):
        for u in range(2):
            for j in range(4):
                flat[pl.ds((first + u * 8) * 8 + h * 4 + j, 8, stride=8), :] = value[
                    u * 8:(u + 1) * 8, j * 128:(j + 1) * 128
                ]

    def picked(h, shard, place, r):
        col = LC[place, r]
        lane = lax.broadcasted_iota(jnp.int32, (CAP, 128), 1)
        hot = jnp.concatenate(
            [jnp.where(col == lane + 128 * t, 1.0, 0.0) for t in range(NODES // 128)], axis=1
        ).astype(jnp.bfloat16)
        return jnp.dot(hot, T[h, shard], preferred_element_type=jnp.float32)

    def launch(item, place):
        h, shard, n = item
        if n >= SLOTS:
            for i in range(4):
                x_copy(i, (h, shard, n - SLOTS)).wait_send()

        @pl.loop(0, NX - 1)
        def _(r):
            stage[n % SLOTS, r] = picked(h, shard, place, r + 1).astype(jnp.bfloat16)

        for i in (2, 3, 0, 1):
            x_copy(i, item).start()
        own = picked(h, shard, place, 0) * 0.5
        for r in range(CAP // 16):
            to_rows(own[r * 16:(r + 1) * 16], h, (shard * NX + x) * CAP + r * 16)

    def forward(item):
        x_copy(2, item).wait_recv()
        x_copy(4, item).start()
        x_copy(3, item).wait_recv()
        x_copy(5, item).start()

    def unpack(item):
        h, shard, n = item
        for i in (0, 1, 4, 5):
            x_copy(i, item).wait_recv()

        for i in range(3):
            first = (shard * NX + lax.rem(x + i + 1, NX)) * CAP

            @pl.loop(0, CAP // 16)
            def _(r):
                value = landing[n, i, pl.ds(pl.multiple_of(r * 16, 16), 16), :]
                to_rows(value.astype(jnp.float32) * 0.5, h, first + r * 16)

    def grid_side(part):
        @pl.loop(part * 3, part * 3 + 3)
        def _(i):
            rows = pl.ds(pl.multiple_of(i * 128, 128), 128)
            for j in range(4):
                value = 0.5 * jnp.dot(
                    embed[rows, :], wdst[:, j * 256:(j + 1) * 256], preferred_element_type=jnp.float32
                )
                for r in range(16):
                    for t in range(2):
                        gs[pl.ds((i * 128 + r * 8) * 8 + j * 2 + t, 8, stride=8), :] = value[
                            r * 8:(r + 1) * 8, t * 128:(t + 1) * 128
                        ]

    L[z] = look[z]
    columns(z, 0)
    items = []
    for h in range(2):
        project(h)
        if h == 0:
            pl.semaphore_wait(barrier, len(peers))
        z_copy(0, 1, h).start()
        z_copy(1, 1, h).start()
        if h == 0:
            for k in range(1, NZ):
                lk_copy(k).start()
        items.append((h, z, h))
        launch(items[-1], 0)

    loads[0].wait()
    loads[1].wait()
    grid_side(0)
    grid_side(1)
    pending, landed = list(items), []
    for d in range(1, 5):
        below, above = lax.rem(z + NZ - d, NZ), lax.rem(z + d, NZ)
        for h in range(2):
            for direction in range(2):
                if d < 4 or direction == h:
                    z_copy(direction, d, h, arriving=True).wait_recv()
                    if d < 3 or (d == 3 and direction == h):
                        z_copy(direction, d + 1, h).start()
            shards = (below, above) if d < 4 else (below,)
            if h == 0:
                for i, shard in enumerate(shards):
                    lk_arrival(shard).wait_recv()
                    columns(shard, 1 + i)
            for item in pending:
                forward(item)
            ready, landed, pending = landed, pending, []
            for i, shard in enumerate(shards):
                items.append((h, shard, len(items)))
                pending.append(items[-1])
                launch(items[-1], 1 + i)
            for item in ready:
                unpack(item)
        if d == 1:
            grid_side(2)
            grid_side(3)
    for item in pending:
        forward(item)
    for item in landed + pending:
        unpack(item)

    for load in loads[2:]:
        load.wait()

    def m_copy(i, b, arriving=False):
        whose, to = [
            (m, up), (m, down), (m, partner),
            (down, up) if b % 2 == 0 else (up, down),
            (down, partner), (up, partner), (far, partner),
        ][i]
        if arriving:
            whose = [down, up, partner, far, down + other, up + other, far + other][i]
        return remote(X.at[whose, b], X.at[whose, b], m_s.at[b * 7 + i], m_r.at[b * 7 + i], member=to)

    def pass_on(b):
        first, second = (0, 1) if b % 2 == 0 else (1, 0)
        m_copy(first, b, True).wait_recv()
        m_copy(3, b).start()
        m_copy(4 + first, b).start()
        m_copy(second, b, True).wait_recv()
        m_copy(4 + second, b).start()

    def pass_far(b):
        m_copy(3, b, True).wait_recv()
        m_copy(6, b).start()

    gain_row = gain[...]
    for b in range(NB):
        @pl.loop(0, PB // 32)
        def _(q):
            for u in range(32):
                p = b * PB + q * 32 + u
                g = gs[pl.ds(pl.multiple_of(p * 8, 8), 8), :]
                total = jnp.zeros((8, 128), jnp.float32)
                for k in range(K):
                    half = F[edge[k, p]] + g
                    total = total + (half + half * jnp.tanh(half))
                S[pl.ds(q * 256 + (u // 8) * 64 + u % 8, 8, stride=8), :] = total

        cube = S[...].reshape(PB // 8, 8, 8, 128)
        summed = jnp.concatenate([cube[:, j].reshape(PB, 128) for j in range(8)], axis=1)
        scale = lax.rsqrt(jnp.mean(summed * summed, axis=-1, keepdims=True) + EPSILON)
        normed = (summed * scale * gain_row).astype(jnp.bfloat16)
        half = 0.5 * jnp.dot(normed, w_node[...], preferred_element_type=jnp.float32)
        hidden = (half + half * jnp.tanh(half)).astype(jnp.bfloat16)
        fields = lax.dot_general(
            w_out[...], hidden, (((1,), (1,)), ((), ())), preferred_element_type=jnp.float32
        )
        point = lax.broadcasted_iota(jnp.int32, (C, PB), 1) + b * PB
        fields = jnp.where(point < rp[0], fields, 0.0).astype(jnp.bfloat16)
        X[m, b, 0:C, :] = fields
        X[m, b, C:CP, :] = jnp.zeros((CP - C, PB), jnp.bfloat16)
        fields_out[:, b * PB:(b + 1) * PB] = fields
        for i in range(3):
            m_copy(i, b).start()
        if b >= 1:
            pass_on(b - 1)
        if b >= 2:
            pass_far(b - 2)

    def slope(v):
        return v * lax.rsqrt(v * v + SOFT_SCALE * SOFT_SCALE)

    wide = jnp.broadcast_to(weight[...], (C, 128))

    def score(b):
        for i in (2, 4, 5, 6):
            m_copy(i, b, True).wait_recv()

        @pl.loop(0, PB // 128)
        def _(t):
            lanes = pl.ds(pl.multiple_of(t * 128, 128), 128)
            whole = pl.ds(pl.multiple_of(b * PB + t * 128, 128), 128)
            here = X[m, b, 0:C, lanes].astype(jnp.float32)
            pair = jnp.zeros((C, 128), jnp.float32)
            for j in range(MEMBERS):
                pair = pair + slope(here - X[j, b, 0:C, lanes].astype(jnp.float32))
            total = slope(here - targets[:, whole]) - pair * (1.0 / (MEMBERS - 1))
            point = lax.broadcasted_iota(jnp.int32, (C, 128), 1) + b * PB + t * 128
            score_out[:, whole] = jnp.where(point < rp[0], wide * total, 0.0)

    score(0)
    pass_on(NB - 1)
    score(1)
    pass_far(NB - 2)
    score(2)
    pass_far(NB - 1)
    for b in range(3, NB):
        score(b)

    for item in items:
        for i in range(6):
            if i >= 4 or item[2] >= len(items) - SLOTS:
                x_copy(i, item).wait_send()
    for d in range(1, 5):
        for h in range(2):
            for direction in range(2):
                if d < 4 or h == direction:
                    z_copy(direction, d, h).wait_send()
    for k in range(1, NZ):
        lk_copy(k).wait_send()
    for b in range(NB):
        for i in range(7):
            m_copy(i, b).wait_send()


def decoder_call(edge, rp, latent, w_src, look, gain, weight, embed, w_dst, w_node, w_out, targets):
    n_items = 2 * NZ
    vm = pl.BlockSpec(memory_space=pltpu.VMEM)
    sm = pl.BlockSpec(memory_space=pltpu.SMEM)
    hbm = pl.BlockSpec(memory_space=pl.ANY)
    dma = pltpu.SemaphoreType.DMA
    half, full = jnp.bfloat16, jnp.float32
    return pl.pallas_call(
        decoder_kernel,
        out_shape=(
            jax.ShapeDtypeStruct((C, G), half),
            jax.ShapeDtypeStruct((C, G), full),
        ),
        in_specs=[sm, sm, vm, vm, vm, vm, vm, hbm, hbm, hbm, hbm, hbm],
        out_specs=(vm, vm),
        scratch_shapes=[
            pltpu.VMEM((2, NZ, NODES, W), half),
            pltpu.VMEM((SLOTS, NX - 1, CAP, W), half),
            pltpu.VMEM((n_items, NX - 1, CAP, W), half),
            pltpu.VMEM((n_items, 64, W), half),
            pltpu.VMEM((n_items, 64, W), half),
            pltpu.VMEM((NZ, NX, CAP), jnp.int32),
            pltpu.VMEM((3, NX, CAP, 128), jnp.int32),
            pltpu.VMEM((ROWS * CAP, 8, 128), full),
            pltpu.VMEM((G * 8, 128), full),
            pltpu.VMEM((PB * 8, 128), full),
            pltpu.VMEM((MEMBERS, NB, CP, PB), half),
            pltpu.VMEM((G, D), half),
            pltpu.VMEM((D, D), half),
            pltpu.VMEM((D, D), half),
            pltpu.VMEM((C, D), half),
            pltpu.VMEM((C, G), full),
            dma((NZ,)), dma((NZ,)),
            dma((16,)), dma((16,)),
            dma((n_items * 6,)), dma((n_items * 6,)),
            dma((NB * 7,)), dma((NB * 7,)),
            dma((5,)),
        ],
        compiler_params=pltpu.CompilerParams(
            collective_id=0, has_side_effects=True, vmem_limit_bytes=VMEM_LIMIT
        ),
        cost_estimate=pl.CostEstimate(flops=14 * 10**9, bytes_accessed=20 * MIB, transcendentals=0),
        name="decoder",
    )(edge, rp, latent, w_src, look, gain, weight, embed, w_dst, w_node, w_out, targets)


def local(
    processed_latent_nodes, grid_embed, dispatch_node_lookup, send_count, edge_slot, row_points,
    w_src, w_dst, gain_node, w_node, w_out, targets, channel_weight,
):
    del send_count
    fields, score = decoder_call(
        edge_slot, row_points, processed_latent_nodes[0], w_src,
        dispatch_node_lookup.reshape(NZ, NX, CAP), gain_node[None, :], channel_weight[:, None],
        grid_embed, w_dst, w_node, w_out, targets,
    )
    return fields[None], score[None]


def solution(mesh):
    placed = (
        P("member", "rows", None),
        P("rows", None),
        P("rows", None),
        P("rows"),
        P(None, "rows"),
        P("rows"),
        P(),
        P(),
        P(),
        P(),
        P(),
        P(None, "rows"),
        P(),
    )
    return jax.shard_map(
        local,
        mesh=mesh,
        in_specs=placed,
        out_specs=(P("member", None, "rows"), P("member", None, "rows")),
        check_vma=False,
    )
```

```python
import functools

import jax
import jax.numpy as jnp
from jax import lax
from jax.experimental import pallas as pl
from jax.experimental.pallas import tpu as pltpu
from jax.sharding import PartitionSpec as P

SOFT_SCALE = 0.5
EPSILON = 1e-05
MESH = pl.DeviceIdType.MESH

NZ, NX, NY = 8, 4, 4
ROWS = NZ * NX
MEMBERS = 8
CAP = 128
NODES = 512
D = 1024
W = 256
Q = D // W
G = 1536
C = 100
CP = 112
K = 3
PB = 256
NB = G // PB
SLOTS = 16
MIB = 1 << 20
VMEM_LIMIT = 60 * MIB


def row_id(z, x):
    return lax.rem(z, NZ) * NX + lax.rem(x, NX)


def decoder_kernel(
    edge, rp, latent, w_src, look, gain, weight,
    embed_hbm, wdst_hbm, wnode_hbm, wout_hbm, targets_hbm,
    fields_out, score_out,
    T, stage, landing, L, hot, F, gs, S, X,
    embed, square, w_out, targets,
    lk_s, lk_r, z_s, z_r, x_s, x_r, m_s, m_r, pre,
):
    me = lax.axis_index("rows")
    z = me // NX
    x = lax.rem(me, NX)
    m = lax.axis_index("member")
    y = m // 2
    c = lax.rem(m, 2)
    north, south = row_id(z + 1, x), row_id(z + NZ - 1, x)

    flat = F.reshape(ROWS * CAP * 8, 128)

    def chip(k):
        return lax.rem(y + k, NY) * 2

    up, down, far, partner = chip(1) + c, chip(3) + c, chip(2) + c, chip(0) + 1 - c
    other = 1 - 2 * c

    barrier = pltpu.get_barrier_semaphore()
    peers = [{"rows": row_id(z + k, x)} for k in range(1, NZ)]
    peers += [{"rows": row_id(z, x + k)} for k in range(1, NX)]
    peers += [{"member": up}, {"member": down}, {"member": partner}]
    for peer in peers:
        pl.semaphore_signal(barrier, inc=1, device_id=peer, device_id_type=MESH)

    loads = [
        pltpu.make_async_copy(a, b, pre.at[i])
        for i, (a, b) in enumerate([
            (embed_hbm, embed), (wdst_hbm, square), (wout_hbm, w_out), (targets_hbm, targets),
        ])
    ]
    for load in loads:
        load.start()
    load_node = pltpu.make_async_copy(wnode_hbm, square, pre.at[4])

    def remote(src, dst, ss, rs, **to):
        return pltpu.make_async_remote_copy(
            src_ref=src, dst_ref=dst, send_sem=ss, recv_sem=rs,
            device_id=to, device_id_type=MESH,
        )

    def project(q):
        T[q, z] = jnp.dot(
            latent[...], w_src[:, q * W:(q + 1) * W], preferred_element_type=jnp.float32
        ).astype(jnp.bfloat16)

    def z_copy(direction, d, q, arriving=False):
        back = d if arriving else d - 1
        shard = lax.rem(z + NZ - back, NZ) if direction == 0 else lax.rem(z + back, NZ)
        i = (direction * 4 + d - 1) * Q + q
        return remote(
            T.at[q, shard], T.at[q, shard], z_s.at[i], z_r.at[i],
            rows=north if direction == 0 else south,
        )

    def goes(direction, d, q):
        return d < 4 or q % 2 == direction

    def lk_copy(k):
        to_z = lax.rem(z + k, NZ)
        return remote(look.at[to_z], L.at[z], lk_s.at[k], lk_r.at[z], rows=row_id(to_z, x))

    def lk_arrival(shard):
        return remote(look.at[shard], L.at[shard], lk_s.at[0], lk_r.at[shard], rows=north)

    def x_copy(i, item):
        n = item[2]
        to = row_id(z, x + 1 + i)
        return remote(
            stage.at[n % SLOTS, i], landing.at[n, 2 - i], x_s.at[n * 3 + i], x_r.at[n * 3 + i], rows=to
        )

    def choose(shard, place):
        for r in range(NX):
            line = jnp.broadcast_to(L[shard, pl.ds(lax.rem(x + r, NX), 1), :], (CAP, 128))
            col = jnp.transpose(line)
            lane = lax.broadcasted_iota(jnp.int32, (CAP, 128), 1)
            for t in range(NODES // 128):
                hot[place, r * CAP:(r + 1) * CAP, t * 128:(t + 1) * 128] = jnp.where(
                    col == lane + 128 * t, 1.0, 0.0
                ).astype(jnp.bfloat16)

    def to_rows(value, q, first):
        for u in range(2):
            for j in range(W // 128):
                flat[pl.ds((first + u * 8) * 8 + q * (W // 128) + j, 8, stride=8), :] = value[
                    u * 8:(u + 1) * 8, j * 128:(j + 1) * 128
                ]

    def launch(item, place):
        q, shard, n = item
        if n >= SLOTS:
            for i in range(NX - 1):
                x_copy(i, (q, shard, n - SLOTS)).wait_send()
        picked = jnp.dot(hot[place], T[q, shard], preferred_element_type=jnp.float32)
        for i in range(NX - 1):
            stage[n % SLOTS, i] = picked[(i + 1) * CAP:(i + 2) * CAP].astype(jnp.bfloat16)
        for i in (1, 0, 2):
            x_copy(i, item).start()
        for r in range(CAP // 16):
            to_rows(picked[r * 16:(r + 1) * 16] * 0.5, q, (shard * NX + x) * CAP + r * 16)

    def unpack(item):
        q, shard, n = item
        for i in range(NX - 1):
            x_copy(i, item).wait_recv()

        for i in range(NX - 1):
            first = (shard * NX + lax.rem(x + i + 1, NX)) * CAP

            @pl.loop(0, CAP // 32)
            def _(r):
                value = landing[n, i, pl.ds(pl.multiple_of(r * 32, 32), 32), :].astype(jnp.float32) * 0.5
                for v in range(2):
                    to_rows(value[v * 16:(v + 1) * 16], q, first + r * 32 + v * 16)

    def grid_side(i):
        for j in range(D // 256):
            value = 0.5 * jnp.dot(
                embed[i * 128:(i + 1) * 128, :], square[:, j * 256:(j + 1) * 256],
                preferred_element_type=jnp.float32,
            )
            for r in range(16):
                for t in range(2):
                    gs[pl.ds((i * 128 + r * 8) * 8 + j * 2 + t, 8, stride=8), :] = value[
                        r * 8:(r + 1) * 8, t * 128:(t + 1) * 128
                    ]

    L[z] = look[z]
    choose(z, 0)
    items = []
    for q in range(Q):
        project(q)
        if q == 0:
            pl.semaphore_wait(barrier, len(peers))
        z_copy(0, 1, q).start()
        z_copy(1, 1, q).start()
        if q == 0:
            for k in range(1, NZ):
                lk_copy(k).start()
        items.append((q, z, q))
        launch(items[-1], 0)

    loads[0].wait()
    loads[1].wait()
    landed = [items[0:2], items[2:4]]
    step = 0
    for d in range(1, 5):
        below, above = lax.rem(z + NZ - d, NZ), lax.rem(z + d, NZ)
        shards = (below, above) if d < 4 else (below,)
        for q in range(Q):
            for direction in range(2):
                if goes(direction, d, q):
                    z_copy(direction, d, q, arriving=True).wait_recv()
                    if d < 4 and goes(direction, d + 1, q):
                        z_copy(direction, d + 1, q).start()
            if q == 0:
                for i, shard in enumerate(shards):
                    lk_arrival(shard).wait_recv()
                    choose(shard, 1 + i)
            new = []
            for i, shard in enumerate(shards):
                items.append((q, shard, len(items)))
                new.append(items[-1])
                launch(items[-1], 1 + i)
            landed.append(new)
            if step < G // 128:
                grid_side(step)
            if step == G // 128:
                load_node.start()
            if len(landed) > 3:
                for item in landed.pop(0):
                    unpack(item)
            step += 1
    for group in landed:
        for item in group:
            unpack(item)

    loads[2].wait()
    loads[3].wait()
    load_node.wait()

    def m_copy(i, b, arriving=False):
        whose, to = [
            (m, up), (m, down), (m, partner),
            (down, up) if b % 2 == 0 else (up, down),
            (down, partner), (up, partner), (far, partner),
        ][i]
        if arriving:
            whose = [down, up, partner, far, down + other, up + other, far + other][i]
        return remote(X.at[whose, b], X.at[whose, b], m_s.at[b * 7 + i], m_r.at[b * 7 + i], member=to)

    def pass_on(b):
        first, second = (0, 1) if b % 2 == 0 else (1, 0)
        m_copy(first, b, True).wait_recv()
        m_copy(3, b).start()
        m_copy(4 + first, b).start()
        m_copy(second, b, True).wait_recv()
        m_copy(4 + second, b).start()

    def pass_far(b):
        m_copy(3, b, True).wait_recv()
        m_copy(6, b).start()

    gain_row = gain[...]
    for b in range(NB):
        @pl.loop(0, PB // 32)
        def _(q):
            for u in range(32):
                p = b * PB + q * 32 + u
                g = gs[pl.ds(pl.multiple_of(p * 8, 8), 8), :]
                total = jnp.zeros((8, 128), jnp.float32)
                for k in range(K):
                    half = F[edge[k, p]] + g
                    total = total + (half + half * jnp.tanh(half))
                S[pl.ds(q * 256 + (u // 8) * 64 + u % 8, 8, stride=8), :] = total

        cube = S[...].reshape(PB // 8, 8, 8, 128)
        summed = jnp.concatenate([cube[:, j].reshape(PB, 128) for j in range(8)], axis=1)
        scale = lax.rsqrt(jnp.mean(summed * summed, axis=-1, keepdims=True) + EPSILON)
        normed = (summed * scale * gain_row).astype(jnp.bfloat16)
        half = 0.5 * jnp.dot(normed, square[...], preferred_element_type=jnp.float32)
        hidden = (half + half * jnp.tanh(half)).astype(jnp.bfloat16)
        fields = lax.dot_general(
            w_out[...], hidden, (((1,), (1,)), ((), ())), preferred_element_type=jnp.float32
        )
        point = lax.broadcasted_iota(jnp.int32, (C, PB), 1) + b * PB
        fields = jnp.where(point < rp[0], fields, 0.0).astype(jnp.bfloat16)
        X[m, b, 0:C, :] = fields
        X[m, b, C:CP, :] = jnp.zeros((CP - C, PB), jnp.bfloat16)
        fields_out[:, b * PB:(b + 1) * PB] = fields
        for i in range(3):
            m_copy(i, b).start()
        if b >= 2:
            pass_on(b - 2)
        if b >= 4:
            pass_far(b - 4)

    def slope(v):
        return v * lax.rsqrt(v * v + SOFT_SCALE * SOFT_SCALE)

    line = jnp.concatenate([weight[...], jnp.zeros((1, 128 - C), jnp.float32)], axis=1)
    wide = jnp.transpose(jnp.broadcast_to(line, (128, 128)))[0:C, :]

    def score(b):
        for i in (2, 4, 5, 6):
            m_copy(i, b, True).wait_recv()

        @pl.loop(0, PB // 128)
        def _(t):
            lanes = pl.ds(pl.multiple_of(t * 128, 128), 128)
            whole = pl.ds(pl.multiple_of(b * PB + t * 128, 128), 128)
            here = X[m, b, 0:C, lanes].astype(jnp.float32)
            pair = jnp.zeros((C, 128), jnp.float32)
            for j in range(MEMBERS):
                pair = pair + slope(here - X[j, b, 0:C, lanes].astype(jnp.float32))
            total = slope(here - targets[:, whole]) - pair * (1.0 / (MEMBERS - 1))
            point = lax.broadcasted_iota(jnp.int32, (C, 128), 1) + b * PB + t * 128
            score_out[:, whole] = jnp.where(point < rp[0], wide * total, 0.0)

    pass_far(NB - 4)
    pass_on(NB - 2)
    score(0)
    pass_far(NB - 3)
    score(1)
    pass_on(NB - 1)
    score(2)
    pass_far(NB - 2)
    score(3)
    pass_far(NB - 1)
    score(4)
    score(5)

    for item in items[-SLOTS:]:
        for i in range(NX - 1):
            x_copy(i, item).wait_send()
    for d in range(1, 5):
        for q in range(Q):
            for direction in range(2):
                if goes(direction, d, q):
                    z_copy(direction, d, q).wait_send()
    for k in range(1, NZ):
        lk_copy(k).wait_send()
    for b in range(NB):
        for i in range(7):
            m_copy(i, b).wait_send()


def decoder_call(edge, rp, latent, w_src, look, gain, weight, embed, w_dst, w_node, w_out, targets):
    n_items = Q * NZ
    vm = pl.BlockSpec(memory_space=pltpu.VMEM)
    sm = pl.BlockSpec(memory_space=pltpu.SMEM)
    hbm = pl.BlockSpec(memory_space=pl.ANY)
    dma = pltpu.SemaphoreType.DMA
    half, full = jnp.bfloat16, jnp.float32
    return pl.pallas_call(
        decoder_kernel,
        out_shape=(
            jax.ShapeDtypeStruct((C, G), half),
            jax.ShapeDtypeStruct((C, G), full),
        ),
        in_specs=[sm, sm, vm, vm, vm, vm, vm, hbm, hbm, hbm, hbm, hbm],
        out_specs=(vm, vm),
        scratch_shapes=[
            pltpu.VMEM((Q, NZ, NODES, W), half),
            pltpu.VMEM((SLOTS, NX - 1, CAP, W), half),
            pltpu.VMEM((n_items, NX - 1, CAP, W), half),
            pltpu.VMEM((NZ, NX, CAP), jnp.int32),
            pltpu.VMEM((3, NX * CAP, NODES), half),
            pltpu.VMEM((ROWS * CAP, 8, 128), full),
            pltpu.VMEM((G * 8, 128), full),
            pltpu.VMEM((PB * 8, 128), full),
            pltpu.VMEM((MEMBERS, NB, CP, PB), half),
            pltpu.VMEM((G, D), half),
            pltpu.VMEM((D, D), half),
            pltpu.VMEM((C, D), half),
            pltpu.VMEM((C, G), full),
            dma((NZ,)), dma((NZ,)),
            dma((8 * Q,)), dma((8 * Q,)),
            dma((n_items * 3,)), dma((n_items * 3,)),
            dma((NB * 7,)), dma((NB * 7,)),
            dma((5,)),
        ],
        compiler_params=pltpu.CompilerParams(
            collective_id=0, has_side_effects=True, vmem_limit_bytes=VMEM_LIMIT
        ),
        cost_estimate=pl.CostEstimate(flops=14 * 10**9, bytes_accessed=20 * MIB, transcendentals=0),
        name="decoder",
    )(edge, rp, latent, w_src, look, gain, weight, embed, w_dst, w_node, w_out, targets)


def local(
    processed_latent_nodes, grid_embed, dispatch_node_lookup, send_count, edge_slot, row_points,
    w_src, w_dst, gain_node, w_node, w_out, targets, channel_weight,
):
    del send_count
    fields, score = decoder_call(
        edge_slot, row_points, processed_latent_nodes[0], w_src,
        dispatch_node_lookup.reshape(NZ, NX, CAP), gain_node[None, :], channel_weight[None, :],
        grid_embed, w_dst, w_node, w_out, targets,
    )
    return fields[None], score[None]


def solution(mesh):
    placed = (
        P("member", "rows", None),
        P("rows", None),
        P("rows", None),
        P("rows"),
        P(None, "rows"),
        P("rows"),
        P(),
        P(),
        P(),
        P(),
        P(),
        P(None, "rows"),
        P(),
    )
    return jax.shard_map(
        local,
        mesh=mesh,
        in_specs=placed,
        out_specs=(P("member", None, "rows"), P("member", None, "rows")),
        check_vma=False,
    )
```

```python
import functools

import jax
import jax.numpy as jnp
from jax import lax
from jax.experimental import pallas as pl
from jax.experimental.pallas import tpu as pltpu
from jax.sharding import PartitionSpec as P

SOFT_SCALE = 0.5
EPSILON = 1e-05
MESH = pl.DeviceIdType.MESH

NZ, NX, NY = 8, 4, 4
ROWS = NZ * NX
MEMBERS = 8
CAP = 128
NODES = 512
D = 1024
W = 256
Q = D // W
G = 1536
C = 100
CP = 112
K = 3
PB = 256
BLOCKS = [(i * PB, PB) for i in range(5)] + [(5 * PB, 128), (5 * PB + 128, 128)]
NB = len(BLOCKS)
SLOTS = 16
MIB = 1 << 20
VMEM_LIMIT = 56 * MIB


def row_id(z, x):
    return lax.rem(z, NZ) * NX + lax.rem(x, NX)


def decoder_kernel(
    edge, look, gain, weight,
    rp_hbm, latent_hbm, wsrc_hbm, embed_hbm, wdst_hbm, wnode_hbm, wout_hbm, targets_hbm,
    fields_out, score_out,
    T, stage, landing, L, hot, F, gs, S, X,
    fields_all, rp, latent, w_src, embed, square, w_out, targets,
    lk_s, lk_r, z_s, z_r, x_s, x_r, m_s, m_r, pre, first,
):
    me = lax.axis_index("rows")
    z = me // NX
    x = lax.rem(me, NX)
    m = lax.axis_index("member")
    y = m // 2
    c = lax.rem(m, 2)
    north, south = row_id(z + 1, x), row_id(z + NZ - 1, x)

    flat = F.reshape(ROWS * CAP * 8, 128)

    def chip(k):
        return lax.rem(y + k, NY) * 2

    up, down, far, partner = chip(1) + c, chip(3) + c, chip(2) + c, chip(0) + 1 - c
    other = 1 - 2 * c

    barrier = pltpu.get_barrier_semaphore()
    peers = [{"rows": row_id(z + k, x)} for k in range(1, NZ)]
    peers += [{"rows": row_id(z, x + k)} for k in range(1, NX)]
    peers += [{"member": lax.rem(m + k, MEMBERS)} for k in range(1, MEMBERS)]
    for peer in peers:
        pl.semaphore_signal(barrier, inc=1, device_id=peer, device_id_type=MESH)

    head = [pltpu.make_async_copy(latent_hbm, latent, first.at[Q])]
    for q in range(Q):
        cols = pl.ds(q * W, W)
        head.append(pltpu.make_async_copy(wsrc_hbm.at[:, cols], w_src.at[q], first.at[q]))
    loads = [
        pltpu.make_async_copy(a, b, pre.at[i])
        for i, (a, b) in enumerate([
            (embed_hbm, embed), (wdst_hbm, square), (wout_hbm, w_out), (targets_hbm, targets), (rp_hbm, rp),
        ])
    ]
    for load in head + loads:
        load.start()
    load_node = pltpu.make_async_copy(wnode_hbm, square, pre.at[5])

    def remote(src, dst, ss, rs, **to):
        return pltpu.make_async_remote_copy(
            src_ref=src, dst_ref=dst, send_sem=ss, recv_sem=rs,
            device_id=to, device_id_type=MESH,
        )

    def project(q):
        T[q, z] = jnp.dot(
            latent[...], w_src[q], preferred_element_type=jnp.float32
        ).astype(jnp.bfloat16)

    def z_copy(direction, d, q, arriving=False):
        back = d if arriving else d - 1
        shard = lax.rem(z + NZ - back, NZ) if direction == 0 else lax.rem(z + back, NZ)
        i = (direction * 4 + d - 1) * Q + q
        return remote(
            T.at[q, shard], T.at[q, shard], z_s.at[i], z_r.at[i],
            rows=north if direction == 0 else south,
        )

    def goes(direction, d, q):
        return d < 4 or q % 2 == direction

    def lk_copy(k):
        to_z = lax.rem(z + k, NZ)
        return remote(look.at[to_z], L.at[z], lk_s.at[k], lk_r.at[z], rows=row_id(to_z, x))

    def lk_arrival(shard):
        return remote(look.at[shard], L.at[shard], lk_s.at[0], lk_r.at[shard], rows=north)

    def x_copy(i, item):
        n = item[2]
        to = row_id(z, x + 1 + i)
        return remote(
            stage.at[n % SLOTS, i], landing.at[n, 2 - i], x_s.at[n * 3 + i], x_r.at[n * 3 + i], rows=to
        )

    def choose(shard, place):
        for r in range(NX):
            line = jnp.broadcast_to(L[shard, pl.ds(lax.rem(x + r, NX), 1), :], (CAP, 128))
            col = jnp.transpose(line)
            lane = lax.broadcasted_iota(jnp.int32, (CAP, 128), 1)
            for t in range(NODES // 128):
                hot[place, r * CAP:(r + 1) * CAP, t * 128:(t + 1) * 128] = jnp.where(
                    col == lane + 128 * t, 1.0, 0.0
                ).astype(jnp.bfloat16)

    def to_rows(value, q, first):
        for u in range(2):
            for j in range(W // 128):
                flat[pl.ds((first + u * 8) * 8 + q * (W // 128) + j, 8, stride=8), :] = value[
                    u * 8:(u + 1) * 8, j * 128:(j + 1) * 128
                ]

    def launch(item, place):
        q, shard, n = item
        if n >= SLOTS:
            for i in range(NX - 1):
                x_copy(i, (q, shard, n - SLOTS)).wait_send()
        picked = jnp.dot(hot[place], T[q, shard], preferred_element_type=jnp.float32)
        for i in range(NX - 1):
            stage[n % SLOTS, i] = picked[(i + 1) * CAP:(i + 2) * CAP].astype(jnp.bfloat16)
        for i in (1, 0, 2):
            x_copy(i, item).start()
        for r in range(CAP // 16):
            to_rows(picked[r * 16:(r + 1) * 16] * 0.5, q, (shard * NX + x) * CAP + r * 16)

    def unpack(item):
        q, shard, n = item
        for i in range(NX - 1):
            x_copy(i, item).wait_recv()

        for i in range(NX - 1):
            first = (shard * NX + lax.rem(x + i + 1, NX)) * CAP

            @pl.loop(0, CAP // 32)
            def _(r):
                value = landing[n, i, pl.ds(pl.multiple_of(r * 32, 32), 32), :].astype(jnp.float32) * 0.5
                for v in range(2):
                    to_rows(value[v * 16:(v + 1) * 16], q, first + r * 32 + v * 16)

    def grid_side(i):
        for j in range(D // 256):
            value = 0.5 * jnp.dot(
                embed[i * 128:(i + 1) * 128, :], square[:, j * 256:(j + 1) * 256],
                preferred_element_type=jnp.float32,
            )
            for r in range(16):
                for t in range(2):
                    gs[pl.ds((i * 128 + r * 8) * 8 + j * 2 + t, 8, stride=8), :] = value[
                        r * 8:(r + 1) * 8, t * 128:(t + 1) * 128
                    ]

    L[z] = look[z]
    choose(z, 0)
    items = []
    head[0].wait()
    for q in range(Q):
        head[1 + q].wait()
        project(q)
        if q == 0:
            pl.semaphore_wait(barrier, len(peers))
        z_copy(0, 1, q).start()
        z_copy(1, 1, q).start()
        if q == 0:
            for k in range(1, NZ):
                lk_copy(k).start()
        items.append((q, z, q))
        launch(items[-1], 0)

    loads[0].wait()
    loads[1].wait()
    landed = [items[0:2], items[2:4]]
    step = 0
    for d in range(1, 5):
        below, above = lax.rem(z + NZ - d, NZ), lax.rem(z + d, NZ)
        shards = (below, above) if d < 4 else (below,)
        for q in range(Q):
            for direction in range(2):
                if goes(direction, d, q):
                    z_copy(direction, d, q, arriving=True).wait_recv()
                    if d < 4 and goes(direction, d + 1, q):
                        z_copy(direction, d + 1, q).start()
            if q == 0:
                for i, shard in enumerate(shards):
                    lk_arrival(shard).wait_recv()
                    choose(shard, 1 + i)
            new = []
            for i, shard in enumerate(shards):
                items.append((q, shard, len(items)))
                new.append(items[-1])
                launch(items[-1], 1 + i)
            landed.append(new)
            if step < G // 128:
                grid_side(step)
            if step == G // 128:
                load_node.start()
            if len(landed) > 3:
                for item in landed.pop(0):
                    unpack(item)
            step += 1
    for group in landed:
        for item in group:
            unpack(item)

    loads[2].wait()
    loads[3].wait()
    loads[4].wait()
    load_node.wait()

    def m_copy(i, b, arriving=False):
        if b == NB - 1:
            whose = m
            to = [up, down, partner, far, up + other, down + other, far + other][i]
        else:
            whose, to = [
                (m, up), (m, down), (m, partner),
                (m, far) if b >= NB - 3 else (down, up) if b % 2 == 0 else (up, down),
                (down, partner), (up, partner), (far, partner),
            ][i]
        if arriving:
            whose = [down, up, partner, far, down + other, up + other, far + other][i]
        spot = X.at[whose, :, pl.ds(*BLOCKS[b])]
        return remote(spot, spot, m_s.at[b * 7 + i], m_r.at[b * 7 + i], member=to)

    def pass_on(b):
        first, second = (0, 1) if b % 2 == 0 else (1, 0)
        m_copy(first, b, True).wait_recv()
        if b < NB - 3:
            m_copy(3, b).start()
        m_copy(4 + first, b).start()
        m_copy(second, b, True).wait_recv()
        m_copy(4 + second, b).start()

    def pass_far(b):
        m_copy(3, b, True).wait_recv()
        m_copy(6, b).start()

    gain_row = gain[...]

    limit = rp[0]
    save_fields = pltpu.make_async_copy(fields_all, fields_out, pre.at[6])

    for b in range(NB):
        start, size = BLOCKS[b]

        @pl.loop(0, size // 32)
        def _(q):
            for u in range(32):
                p = start + q * 32 + u
                g = gs[pl.ds(pl.multiple_of(p * 8, 8), 8), :]
                total = jnp.zeros((8, 128), jnp.float32)
                for k in range(K):
                    half = F[edge[k, p]] + g
                    total = total + (half + half * jnp.tanh(half))
                S[pl.ds(q * 256 + (u // 8) * 64 + u % 8, 8, stride=8), :] = total

        cube = S[0:size * 8, :].reshape(size // 8, 8, 8, 128)
        summed = jnp.concatenate([cube[:, j].reshape(size, 128) for j in range(8)], axis=1)
        scale = lax.rsqrt(jnp.mean(summed * summed, axis=-1, keepdims=True) + EPSILON)
        normed = (summed * scale * gain_row).astype(jnp.bfloat16)
        half = 0.5 * jnp.dot(normed, square[...], preferred_element_type=jnp.float32)
        hidden = (half + half * jnp.tanh(half)).astype(jnp.bfloat16)
        fields = lax.dot_general(
            w_out[...], hidden, (((1,), (1,)), ((), ())), preferred_element_type=jnp.float32
        )
        point = lax.broadcasted_iota(jnp.int32, (C, size), 1) + start
        fields = jnp.where(point < limit, fields, 0.0).astype(jnp.bfloat16)
        X[m, 0:C, start:start + size] = fields
        X[m, C:CP, start:start + size] = jnp.zeros((CP - C, size), jnp.bfloat16)
        for i in range(7 if b == NB - 1 else 4 if b >= NB - 3 else 3):
            m_copy(i, b).start()
        fields_all[:, start:start + size] = fields
        if b == NB - 1:
            save_fields.start()
        if b >= 2:
            pass_on(b - 2)
        if b >= 4:
            pass_far(b - 4)

    def slope(v):
        return v * lax.rsqrt(v * v + SOFT_SCALE * SOFT_SCALE)

    line = jnp.concatenate([weight[...], jnp.zeros((1, 128 - C), jnp.float32)], axis=1)
    wide = jnp.transpose(jnp.broadcast_to(line, (128, 128)))[0:C, :]

    def score(b):
        start, size = BLOCKS[b]
        for i in (range(7) if b == NB - 1 else (2, 4, 5, 6)):
            m_copy(i, b, True).wait_recv()

        @pl.loop(0, size // 128)
        def _(t):
            tile = start // 128 + t
            lanes = pl.ds(pl.multiple_of(tile * 128, 128), 128)
            here = X[m, 0:C, lanes].astype(jnp.float32)
            pair = jnp.zeros((C, 128), jnp.float32)
            for k in range(1, MEMBERS):
                pair = pair + slope(here - X[lax.rem(m + k, MEMBERS), 0:C, lanes].astype(jnp.float32))
            total = slope(here - targets[:, lanes]) - pair * (1.0 / (MEMBERS - 1))
            point = lax.broadcasted_iota(jnp.int32, (C, 128), 1) + tile * 128
            score_out[pl.ds(tile, C, stride=G // 128), :] = jnp.where(point < limit, wide * total, 0.0)

    pass_far(NB - 4)
    score(0)
    pass_far(NB - 3)
    pass_on(NB - 2)
    score(1)
    pass_far(NB - 2)
    for b in range(2, NB):
        score(b)

    for item in items[-SLOTS:]:
        for i in range(NX - 1):
            x_copy(i, item).wait_send()
    for d in range(1, 5):
        for q in range(Q):
            for direction in range(2):
                if goes(direction, d, q):
                    z_copy(direction, d, q).wait_send()
    for k in range(1, NZ):
        lk_copy(k).wait_send()
    for b in range(NB):
        for i in range(7):
            m_copy(i, b).wait_send()
    save_fields.wait()


def decoder_call(edge, look, gain, weight, *arrays):
    n_items = Q * NZ
    vm = pl.BlockSpec(memory_space=pltpu.VMEM)
    sm = pl.BlockSpec(memory_space=pltpu.SMEM)
    hbm = pl.BlockSpec(memory_space=pltpu.HBM)
    dma = pltpu.SemaphoreType.DMA
    half, full = jnp.bfloat16, jnp.float32
    return pl.pallas_call(
        decoder_kernel,
        out_shape=(
            jax.ShapeDtypeStruct((C, G), half),
            jax.ShapeDtypeStruct((C * (G // 128), 128), full),
        ),
        in_specs=[sm, vm, vm, vm] + [hbm] * len(arrays),
        out_specs=(hbm, vm),
        scratch_shapes=[
            pltpu.VMEM((Q, NZ, NODES, W), half),
            pltpu.VMEM((SLOTS, NX - 1, CAP, W), half),
            pltpu.VMEM((n_items, NX - 1, CAP, W), half),
            pltpu.VMEM((NZ, NX, CAP), jnp.int32),
            pltpu.VMEM((3, NX * CAP, NODES), half),
            pltpu.VMEM((ROWS * CAP, 8, 128), full),
            pltpu.VMEM((G * 8, 128), full),
            pltpu.VMEM((PB * 8, 128), full),
            pltpu.VMEM((MEMBERS, CP, G), half),
            pltpu.VMEM((C, G), half),
            pltpu.SMEM((1,), jnp.int32),
            pltpu.VMEM((NODES, D), half),
            pltpu.VMEM((Q, D, W), half),
            pltpu.VMEM((G, D), half),
            pltpu.VMEM((D, D), half),
            pltpu.VMEM((C, D), half),
            pltpu.VMEM((C, G), full),
            dma((NZ,)), dma((NZ,)),
            dma((8 * Q,)), dma((8 * Q,)),
            dma((n_items * 3,)), dma((n_items * 3,)),
            dma((NB * 7,)), dma((NB * 7,)),
            dma((7,)), dma((Q + 1,)),
        ],
        compiler_params=pltpu.CompilerParams(
            collective_id=0, has_side_effects=True, vmem_limit_bytes=VMEM_LIMIT
        ),
        cost_estimate=pl.CostEstimate(flops=14 * 10**9, bytes_accessed=20 * MIB, transcendentals=0),
        name="decoder",
    )(edge, look, gain, weight, *arrays)


def place_kernel(a, b, a_out, b_out, sems):
    copies = [
        pltpu.make_async_copy(a, a_out, sems.at[0]),
        pltpu.make_async_copy(b, b_out, sems.at[1]),
    ]
    for copy in copies:
        copy.start()
    for copy in copies:
        copy.wait()


def place_call(a, b):
    vm = pl.BlockSpec(memory_space=pltpu.VMEM)
    hbm = pl.BlockSpec(memory_space=pltpu.HBM)
    return pl.pallas_call(
        place_kernel,
        out_shape=(jax.ShapeDtypeStruct(a.shape, a.dtype), jax.ShapeDtypeStruct(b.shape, b.dtype)),
        in_specs=[vm, vm],
        out_specs=(hbm, hbm),
        scratch_shapes=[pltpu.SemaphoreType.DMA((2,))],
        name="place",
    )(a, b)


def local(
    processed_latent_nodes, grid_embed, dispatch_node_lookup, send_count, edge_slot, row_points,
    w_src, w_dst, gain_node, w_node, w_out, targets, channel_weight,
):
    del send_count
    fields, score = decoder_call(
        edge_slot, dispatch_node_lookup.reshape(NZ, NX, CAP),
        gain_node[None, :], channel_weight[None, :],
        row_points, processed_latent_nodes[0], w_src, grid_embed, w_dst, w_node, w_out, targets,
    )
    fields, score = place_call(fields, score)
    return fields[None], score.reshape(1, C, G)


def solution(mesh):
    placed = (
        P("member", "rows", None),
        P("rows", None),
        P("rows", None),
        P("rows"),
        P(None, "rows"),
        P("rows"),
        P(),
        P(),
        P(),
        P(),
        P(),
        P(None, "rows"),
        P(),
    )
    return jax.shard_map(
        local,
        mesh=mesh,
        in_specs=placed,
        out_specs=(P("member", None, "rows"), P("member", None, "rows")),
        check_vma=False,
    )
```

```python
import functools

import jax
import jax.numpy as jnp
from jax import lax
from jax.experimental import pallas as pl
from jax.experimental.pallas import tpu as pltpu
from jax.sharding import PartitionSpec as P

SOFT_SCALE = 0.5
EPSILON = 1e-05
MESH = pl.DeviceIdType.MESH

NZ, NX, NY = 8, 4, 4
ROWS = NZ * NX
MEMBERS = 8
CAP = 128
NODES = 512
D = 1024
W = 256
Q = D // W
G = 1536
C = 100
CP = 112
K = 3
PB = 256
BLOCKS = [(i * PB, PB) for i in range(5)] + [(5 * PB, 128), (5 * PB + 128, 128)]
NB = len(BLOCKS)
SLOTS = 16
MIB = 1 << 20
VMEM_LIMIT = 56 * MIB


def row_id(z, x):
    return lax.rem(z, NZ) * NX + lax.rem(x, NX)


def decoder_kernel(
    edge, look, gain, weight,
    rp_hbm, latent_hbm, wsrc_hbm, embed_hbm, wdst_hbm, wnode_hbm, wout_hbm, targets_hbm,
    fields_out, score_out,
    T, stage, landing, L, hot, F, gs, S, X,
    fields_all, order, slots, rp, latent, w_src, embed, square, w_out, targets,
    lk_s, lk_r, z_s, z_r, x_s, x_r, m_s, m_r, pre, first,
):
    me = lax.axis_index("rows")
    z = me // NX
    x = lax.rem(me, NX)
    m = lax.axis_index("member")
    y = m // 2
    c = lax.rem(m, 2)
    north, south = row_id(z + 1, x), row_id(z + NZ - 1, x)

    flat = F.reshape(ROWS * CAP * 8, 128)

    def chip(k):
        return lax.rem(y + k, NY) * 2

    up, down, far, partner = chip(1) + c, chip(3) + c, chip(2) + c, chip(0) + 1 - c
    other = 1 - 2 * c

    barrier = pltpu.get_barrier_semaphore()
    peers = [{"rows": row_id(z + k, x)} for k in range(1, NZ)]
    peers += [{"rows": row_id(z, x + k)} for k in range(1, NX)]
    peers += [{"member": lax.rem(m + k, MEMBERS)} for k in range(1, MEMBERS)]
    for peer in peers:
        pl.semaphore_signal(barrier, inc=1, device_id=peer, device_id_type=MESH)

    head = [pltpu.make_async_copy(latent_hbm, latent, first.at[Q])]
    for q in range(Q):
        cols = pl.ds(q * W, W)
        head.append(pltpu.make_async_copy(wsrc_hbm.at[:, cols], w_src.at[q], first.at[q]))
    loads = [
        pltpu.make_async_copy(a, b, pre.at[i])
        for i, (a, b) in enumerate([
            (embed_hbm, embed), (wdst_hbm, square), (wout_hbm, w_out), (targets_hbm, targets), (rp_hbm, rp),
        ])
    ]
    for load in head + loads:
        load.start()
    load_node = pltpu.make_async_copy(wnode_hbm, square, pre.at[5])

    def remote(src, dst, ss, rs, **to):
        return pltpu.make_async_remote_copy(
            src_ref=src, dst_ref=dst, send_sem=ss, recv_sem=rs,
            device_id=to, device_id_type=MESH,
        )

    def project(q):
        T[q, z] = jnp.dot(
            latent[...], w_src[q], preferred_element_type=jnp.float32
        ).astype(jnp.bfloat16)

    def z_copy(direction, d, q, arriving=False):
        back = d if arriving else d - 1
        shard = lax.rem(z + NZ - back, NZ) if direction == 0 else lax.rem(z + back, NZ)
        i = (direction * 4 + d - 1) * Q + q
        return remote(
            T.at[q, shard], T.at[q, shard], z_s.at[i], z_r.at[i],
            rows=north if direction == 0 else south,
        )

    def goes(direction, d, q):
        return d < 4 or q % 2 == direction

    def lk_copy(k):
        to_z = lax.rem(z + k, NZ)
        return remote(look.at[to_z], L.at[z], lk_s.at[k], lk_r.at[z], rows=row_id(to_z, x))

    def lk_arrival(shard):
        return remote(look.at[shard], L.at[shard], lk_s.at[0], lk_r.at[shard], rows=north)

    def x_copy(i, item):
        n = item[2]
        to = row_id(z, x + 1 + i)
        return remote(
            stage.at[n % SLOTS, i], landing.at[n, 2 - i], x_s.at[n * 3 + i], x_r.at[n * 3 + i], rows=to
        )

    def choose(shard, place):
        for r in range(NX):
            line = jnp.broadcast_to(L[shard, pl.ds(lax.rem(x + r, NX), 1), :], (CAP, 128))
            col = jnp.transpose(line)
            lane = lax.broadcasted_iota(jnp.int32, (CAP, 128), 1)
            for t in range(NODES // 128):
                hot[place, r * CAP:(r + 1) * CAP, t * 128:(t + 1) * 128] = jnp.where(
                    col == lane + 128 * t, 1.0, 0.0
                ).astype(jnp.bfloat16)

    def to_rows(value, q, first):
        for u in range(2):
            for j in range(W // 128):
                flat[pl.ds((first + u * 8) * 8 + q * (W // 128) + j, 8, stride=8), :] = value[
                    u * 8:(u + 1) * 8, j * 128:(j + 1) * 128
                ]

    def launch(item, place):
        q, shard, n = item
        if n >= SLOTS:
            for i in range(NX - 1):
                x_copy(i, (q, shard, n - SLOTS)).wait_send()
        picked = jnp.dot(hot[place], T[q, shard], preferred_element_type=jnp.float32)
        for i in range(NX - 1):
            stage[n % SLOTS, i] = picked[(i + 1) * CAP:(i + 2) * CAP].astype(jnp.bfloat16)
        for i in (1, 0, 2):
            x_copy(i, item).start()
        for r in range(CAP // 16):
            to_rows(picked[r * 16:(r + 1) * 16] * 0.5, q, (shard * NX + x) * CAP + r * 16)

    def unpack(item):
        q, shard, n = item
        for i in range(NX - 1):
            x_copy(i, item).wait_recv()

        for i in range(NX - 1):
            first = (shard * NX + lax.rem(x + i + 1, NX)) * CAP

            @pl.loop(0, CAP // 32)
            def _(r):
                value = landing[n, i, pl.ds(pl.multiple_of(r * 32, 32), 32), :].astype(jnp.float32) * 0.5
                for v in range(2):
                    to_rows(value[v * 16:(v + 1) * 16], q, first + r * 32 + v * 16)

    def grid_side(i):
        for j in range(D // 256):
            value = 0.5 * jnp.dot(
                embed[i * 128:(i + 1) * 128, :], square[:, j * 256:(j + 1) * 256],
                preferred_element_type=jnp.float32,
            )
            for r in range(16):
                for t in range(2):
                    gs[pl.ds((i * 128 + r * 8) * 8 + j * 2 + t, 8, stride=8), :] = value[
                        r * 8:(r + 1) * 8, t * 128:(t + 1) * 128
                    ]

    L[z] = look[z]
    choose(z, 0)
    items = []
    head[0].wait()
    for q in range(Q):
        head[1 + q].wait()
        project(q)
        if q == 0:
            pl.semaphore_wait(barrier, len(peers))
        z_copy(0, 1, q).start()
        z_copy(1, 1, q).start()
        items.append((q, z, q))
        launch(items[-1], 0)
        if q == 0:
            for k in range(1, NZ):
                lk_copy(k).start()

    for row in range(G // 32):
        parts = [edge[k:k + 1, row * 32:(row + 1) * 32] for k in range(K)]
        order[row:row + 1, :] = jnp.concatenate(parts + [jnp.zeros((1, 32), jnp.int32)], axis=1)
    load_slots = pltpu.make_async_copy(order, slots, pre.at[7])
    load_slots.start()

    loads[0].wait()
    loads[1].wait()
    landed = [items[0:2], items[2:4]]
    step = 0
    for d in range(1, 5):
        below, above = lax.rem(z + NZ - d, NZ), lax.rem(z + d, NZ)
        shards = (below, above) if d < 4 else (below,)
        for q in range(Q):
            for direction in range(2):
                if goes(direction, d, q):
                    z_copy(direction, d, q, arriving=True).wait_recv()
                    if d < 4 and goes(direction, d + 1, q):
                        z_copy(direction, d + 1, q).start()
            if q == 0:
                for i, shard in enumerate(shards):
                    lk_arrival(shard).wait_recv()
                    choose(shard, 1 + i)
            new = []
            for i, shard in enumerate(shards):
                items.append((q, shard, len(items)))
                new.append(items[-1])
                launch(items[-1], 1 + i)
            landed.append(new)
            if step < G // 128:
                grid_side(step)
            if step == G // 128:
                load_node.start()
            if len(landed) > 3:
                for item in landed.pop(0):
                    unpack(item)
            step += 1
    for group in landed:
        for item in group:
            unpack(item)

    loads[2].wait()
    loads[3].wait()
    loads[4].wait()
    load_node.wait()
    load_slots.wait()

    def m_copy(i, b, arriving=False):
        if b == NB - 1:
            whose = m
            to = [up, down, partner, far, up + other, down + other, far + other][i]
        else:
            whose, to = [
                (m, up), (m, down), (m, partner),
                (m, far) if b >= NB - 3 else (down, up) if b % 2 == 0 else (up, down),
                (down, partner), (up, partner), (far, partner),
            ][i]
        if arriving:
            whose = [down, up, partner, far, down + other, up + other, far + other][i]
        spot = X.at[whose, :, pl.ds(*BLOCKS[b])]
        return remote(spot, spot, m_s.at[b * 7 + i], m_r.at[b * 7 + i], member=to)

    def pass_on(b):
        first, second = (0, 1) if b % 2 == 0 else (1, 0)
        m_copy(first, b, True).wait_recv()
        if b < NB - 3:
            m_copy(3, b).start()
        m_copy(4 + first, b).start()
        m_copy(second, b, True).wait_recv()
        m_copy(4 + second, b).start()

    def pass_far(b):
        m_copy(3, b, True).wait_recv()
        m_copy(6, b).start()

    gain_row = gain[...]

    limit = rp[0]
    save_fields = pltpu.make_async_copy(fields_all, fields_out, pre.at[6])

    for b in range(NB):
        start, size = BLOCKS[b]

        @pl.loop(0, size // 32)
        def _(q):
            for u in range(32):
                p = start + q * 32 + u
                g = gs[pl.ds(pl.multiple_of(p * 8, 8), 8), :]
                total = jnp.zeros((8, 128), jnp.float32)
                for k in range(K):
                    half = F[slots[start // 32 + q, k * 32 + u]] + g
                    total = total + (half + half * jnp.tanh(half))
                S[pl.ds(q * 256 + (u // 8) * 64 + u % 8, 8, stride=8), :] = total

        cube = S[0:size * 8, :].reshape(size // 8, 8, 8, 128)
        summed = jnp.concatenate([cube[:, j].reshape(size, 128) for j in range(8)], axis=1)
        scale = lax.rsqrt(jnp.mean(summed * summed, axis=-1, keepdims=True) + EPSILON)
        normed = (summed * scale * gain_row).astype(jnp.bfloat16)
        half = 0.5 * jnp.dot(normed, square[...], preferred_element_type=jnp.float32)
        hidden = (half + half * jnp.tanh(half)).astype(jnp.bfloat16)
        fields = lax.dot_general(
            w_out[...], hidden, (((1,), (1,)), ((), ())), preferred_element_type=jnp.float32
        )
        point = lax.broadcasted_iota(jnp.int32, (C, size), 1) + start
        fields = jnp.where(point < limit, fields, 0.0).astype(jnp.bfloat16)
        X[m, 0:C, start:start + size] = fields
        X[m, C:CP, start:start + size] = jnp.zeros((CP - C, size), jnp.bfloat16)
        for i in range(7 if b == NB - 1 else 4 if b >= NB - 3 else 3):
            m_copy(i, b).start()
        fields_all[:, start:start + size] = fields
        if b == NB - 1:
            save_fields.start()
        if b >= 2:
            pass_on(b - 2)
        if b >= 4:
            pass_far(b - 4)

    def slope(v):
        return v * lax.rsqrt(v * v + SOFT_SCALE * SOFT_SCALE)

    line = jnp.concatenate([weight[...], jnp.zeros((1, 128 - C), jnp.float32)], axis=1)
    wide = jnp.transpose(jnp.broadcast_to(line, (128, 128)))[0:C, :]

    def score(b):
        start, size = BLOCKS[b]
        for i in (range(7) if b == NB - 1 else (2, 4, 5, 6)):
            m_copy(i, b, True).wait_recv()

        @pl.loop(0, size // 128)
        def _(t):
            tile = start // 128 + t
            lanes = pl.ds(pl.multiple_of(tile * 128, 128), 128)
            here = X[m, 0:C, lanes].astype(jnp.float32)
            pair = jnp.zeros((C, 128), jnp.float32)
            for k in range(1, MEMBERS):
                pair = pair + slope(here - X[lax.rem(m + k, MEMBERS), 0:C, lanes].astype(jnp.float32))
            total = slope(here - targets[:, lanes]) - pair * (1.0 / (MEMBERS - 1))
            point = lax.broadcasted_iota(jnp.int32, (C, 128), 1) + tile * 128
            score_out[pl.ds(tile, C, stride=G // 128), :] = jnp.where(point < limit, wide * total, 0.0)

    pass_far(NB - 4)
    score(0)
    pass_far(NB - 3)
    pass_on(NB - 2)
    score(1)
    pass_far(NB - 2)
    for b in range(2, NB):
        score(b)

    for item in items[-SLOTS:]:
        for i in range(NX - 1):
            x_copy(i, item).wait_send()
    for d in range(1, 5):
        for q in range(Q):
            for direction in range(2):
                if goes(direction, d, q):
                    z_copy(direction, d, q).wait_send()
    for k in range(1, NZ):
        lk_copy(k).wait_send()
    for b in range(NB):
        for i in range(7):
            m_copy(i, b).wait_send()
    save_fields.wait()


def decoder_call(edge, look, gain, weight, *arrays):
    n_items = Q * NZ
    vm = pl.BlockSpec(memory_space=pltpu.VMEM)
    hbm = pl.BlockSpec(memory_space=pltpu.HBM)
    dma = pltpu.SemaphoreType.DMA
    half, full = jnp.bfloat16, jnp.float32
    return pl.pallas_call(
        decoder_kernel,
        out_shape=(
            jax.ShapeDtypeStruct((C, G), half),
            jax.ShapeDtypeStruct((C * (G // 128), 128), full),
        ),
        in_specs=[vm, vm, vm, vm] + [hbm] * len(arrays),
        out_specs=(hbm, vm),
        scratch_shapes=[
            pltpu.VMEM((Q, NZ, NODES, W), half),
            pltpu.VMEM((SLOTS, NX - 1, CAP, W), half),
            pltpu.VMEM((n_items, NX - 1, CAP, W), half),
            pltpu.VMEM((NZ, NX, CAP), jnp.int32),
            pltpu.VMEM((3, NX * CAP, NODES), half),
            pltpu.VMEM((ROWS * CAP, 8, 128), full),
            pltpu.VMEM((G * 8, 128), full),
            pltpu.VMEM((PB * 8, 128), full),
            pltpu.VMEM((MEMBERS, CP, G), half),
            pltpu.VMEM((C, G), half),
            pltpu.VMEM((G // 32, 128), jnp.int32),
            pltpu.SMEM((G // 32, 128), jnp.int32),
            pltpu.SMEM((1,), jnp.int32),
            pltpu.VMEM((NODES, D), half),
            pltpu.VMEM((Q, D, W), half),
            pltpu.VMEM((G, D), half),
            pltpu.VMEM((D, D), half),
            pltpu.VMEM((C, D), half),
            pltpu.VMEM((C, G), full),
            dma((NZ,)), dma((NZ,)),
            dma((8 * Q,)), dma((8 * Q,)),
            dma((n_items * 3,)), dma((n_items * 3,)),
            dma((NB * 7,)), dma((NB * 7,)),
            dma((8,)), dma((Q + 1,)),
        ],
        compiler_params=pltpu.CompilerParams(
            collective_id=0, has_side_effects=True, vmem_limit_bytes=VMEM_LIMIT
        ),
        cost_estimate=pl.CostEstimate(flops=14 * 10**9, bytes_accessed=20 * MIB, transcendentals=0),
        name="decoder",
    )(edge, look, gain, weight, *arrays)


def place_kernel(a, b, a_out, b_out, sems):
    copies = [
        pltpu.make_async_copy(a, a_out, sems.at[0]),
        pltpu.make_async_copy(b, b_out, sems.at[1]),
    ]
    for copy in copies:
        copy.start()
    for copy in copies:
        copy.wait()


def place_call(a, b):
    vm = pl.BlockSpec(memory_space=pltpu.VMEM)
    hbm = pl.BlockSpec(memory_space=pltpu.HBM)
    return pl.pallas_call(
        place_kernel,
        out_shape=(jax.ShapeDtypeStruct(a.shape, a.dtype), jax.ShapeDtypeStruct(b.shape, b.dtype)),
        in_specs=[vm, vm],
        out_specs=(hbm, hbm),
        scratch_shapes=[pltpu.SemaphoreType.DMA((2,))],
        name="place",
    )(a, b)


def local(
    processed_latent_nodes, grid_embed, dispatch_node_lookup, send_count, edge_slot, row_points,
    w_src, w_dst, gain_node, w_node, w_out, targets, channel_weight,
):
    del send_count
    fields, score = decoder_call(
        edge_slot, dispatch_node_lookup.reshape(NZ, NX, CAP),
        gain_node[None, :], channel_weight[None, :],
        row_points, processed_latent_nodes[0], w_src, grid_embed, w_dst, w_node, w_out, targets,
    )
    fields, score = place_call(fields, score)
    return fields[None], score.reshape(1, C, G)


def solution(mesh):
    placed = (
        P("member", "rows", None),
        P("rows", None),
        P("rows", None),
        P("rows"),
        P(None, "rows"),
        P("rows"),
        P(),
        P(),
        P(),
        P(),
        P(),
        P(None, "rows"),
        P(),
    )
    return jax.shard_map(
        local,
        mesh=mesh,
        in_specs=placed,
        out_specs=(P("member", None, "rows"), P("member", None, "rows")),
        check_vma=False,
    )
```

```python
import functools

import jax
import jax.numpy as jnp
from jax import lax
from jax.experimental import pallas as pl
from jax.experimental.pallas import tpu as pltpu
from jax.sharding import PartitionSpec as P

SOFT_SCALE = 0.5
EPSILON = 1e-05
MESH = pl.DeviceIdType.MESH

NZ, NX, NY = 8, 4, 4
ROWS = NZ * NX
MEMBERS = 8
CAP = 128
NODES = 512
D = 1024
W = 256
Q = D // W
G = 1536
C = 100
CP = 112
K = 3
PB = 256
BLOCKS = [(i * PB, PB) for i in range(5)] + [(5 * PB, 128), (5 * PB + 128, 128)]
NB = len(BLOCKS)
SLOTS = 16
MIB = 1 << 20
VMEM_LIMIT = 56 * MIB


def row_id(z, x):
    return lax.rem(z, NZ) * NX + lax.rem(x, NX)


def decoder_kernel(
    edge, look, gain, weight,
    rp_hbm, latent_hbm, wsrc_hbm, embed_hbm, wdst_hbm, wnode_hbm, wout_hbm, targets_hbm,
    fields_out, score_out,
    T, stage, landing, L, hot, F, gs, S, X,
    fields_all, order, slots, rp, latent, w_src, embed, square, w_out, targets,
    lk_s, lk_r, z_s, z_r, x_s, x_r, m_s, m_r, pre, first,
):
    me = lax.axis_index("rows")
    z = me // NX
    x = lax.rem(me, NX)
    m = lax.axis_index("member")
    y = m // 2
    c = lax.rem(m, 2)
    north, south = row_id(z + 1, x), row_id(z + NZ - 1, x)

    flat = F.reshape(ROWS * CAP * 8, 128)

    def chip(k):
        return lax.rem(y + k, NY) * 2

    up, down, far, partner = chip(1) + c, chip(3) + c, chip(2) + c, chip(0) + 1 - c
    other = 1 - 2 * c

    barrier = pltpu.get_barrier_semaphore()
    peers = [{"rows": row_id(z + k, x)} for k in range(1, NZ)]
    peers += [{"rows": row_id(z, x + k)} for k in range(1, NX)]
    peers += [{"member": lax.rem(m + k, MEMBERS)} for k in range(1, MEMBERS)]
    for peer in peers:
        pl.semaphore_signal(barrier, inc=1, device_id=peer, device_id_type=MESH)

    head = [pltpu.make_async_copy(latent_hbm, latent, first.at[Q])]
    for q in range(Q):
        cols = pl.ds(q * W, W)
        head.append(pltpu.make_async_copy(wsrc_hbm.at[:, cols], w_src.at[q], first.at[q]))
    loads = [
        pltpu.make_async_copy(a, b, pre.at[i])
        for i, (a, b) in enumerate([
            (embed_hbm, embed), (wdst_hbm, square), (wout_hbm, w_out), (targets_hbm, targets), (rp_hbm, rp),
        ])
    ]
    for load in head + loads:
        load.start()
    load_node = pltpu.make_async_copy(wnode_hbm, square, pre.at[5])

    def remote(src, dst, ss, rs, **to):
        return pltpu.make_async_remote_copy(
            src_ref=src, dst_ref=dst, send_sem=ss, recv_sem=rs,
            device_id=to, device_id_type=MESH,
        )

    def project(q):
        T[q, z] = jnp.dot(
            latent[...], w_src[q], preferred_element_type=jnp.float32
        ).astype(jnp.bfloat16)

    def z_copy(direction, d, q, arriving=False):
        back = d if arriving else d - 1
        shard = lax.rem(z + NZ - back, NZ) if direction == 0 else lax.rem(z + back, NZ)
        i = (direction * 4 + d - 1) * Q + q
        return remote(
            T.at[q, shard], T.at[q, shard], z_s.at[i], z_r.at[i],
            rows=north if direction == 0 else south,
        )

    def goes(direction, d, q):
        return d < 4 or q % 2 == direction

    def lk_copy(k):
        to_z = lax.rem(z + k, NZ)
        return remote(look.at[to_z], L.at[z], lk_s.at[k], lk_r.at[z], rows=row_id(to_z, x))

    def lk_arrival(shard):
        return remote(look.at[shard], L.at[shard], lk_s.at[0], lk_r.at[shard], rows=north)

    def x_copy(i, item):
        n = item[2]
        to = row_id(z, x + 1 + i)
        return remote(
            stage.at[n % SLOTS, i], landing.at[n, 2 - i], x_s.at[n * 3 + i], x_r.at[n * 3 + i], rows=to
        )

    def choose(shard, place):
        for r in range(NX):
            line = jnp.broadcast_to(L[shard, pl.ds(lax.rem(x + r, NX), 1), :], (CAP, 128))
            col = jnp.transpose(line)
            lane = lax.broadcasted_iota(jnp.int32, (CAP, 128), 1)
            for t in range(NODES // 128):
                hot[place, r * CAP:(r + 1) * CAP, t * 128:(t + 1) * 128] = jnp.where(
                    col == lane + 128 * t, 1.0, 0.0
                ).astype(jnp.bfloat16)

    def to_rows(value, q, first):
        for u in range(2):
            for j in range(W // 128):
                flat[pl.ds((first + u * 8) * 8 + q * (W // 128) + j, 8, stride=8), :] = value[
                    u * 8:(u + 1) * 8, j * 128:(j + 1) * 128
                ]

    def launch(item, place):
        q, shard, n = item
        if n >= SLOTS:
            for i in range(NX - 1):
                x_copy(i, (q, shard, n - SLOTS)).wait_send()
        picked = jnp.dot(hot[place], T[q, shard], preferred_element_type=jnp.float32)
        for i in range(NX - 1):
            stage[n % SLOTS, i] = picked[(i + 1) * CAP:(i + 2) * CAP].astype(jnp.bfloat16)
        for i in (1, 0, 2):
            x_copy(i, item).start()
        for r in range(CAP // 16):
            to_rows(picked[r * 16:(r + 1) * 16] * 0.5, q, (shard * NX + x) * CAP + r * 16)

    def unpack(item):
        q, shard, n = item
        for i in range(NX - 1):
            x_copy(i, item).wait_recv()

        for i in range(NX - 1):
            first = (shard * NX + lax.rem(x + i + 1, NX)) * CAP

            @pl.loop(0, CAP // 32)
            def _(r):
                value = landing[n, i, pl.ds(pl.multiple_of(r * 32, 32), 32), :].astype(jnp.float32) * 0.5
                for v in range(2):
                    to_rows(value[v * 16:(v + 1) * 16], q, first + r * 32 + v * 16)

    def grid_side(i):
        for j in range(D // 256):
            value = 0.5 * jnp.dot(
                embed[i * 128:(i + 1) * 128, :], square[:, j * 256:(j + 1) * 256],
                preferred_element_type=jnp.float32,
            )
            for r in range(16):
                for t in range(2):
                    gs[pl.ds((i * 128 + r * 8) * 8 + j * 2 + t, 8, stride=8), :] = value[
                        r * 8:(r + 1) * 8, t * 128:(t + 1) * 128
                    ]

    L[z] = look[z]
    choose(z, 0)
    items = []
    head[0].wait()
    for q in range(Q):
        head[1 + q].wait()
        project(q)
        if q == 0:
            pl.semaphore_wait(barrier, len(peers))
        z_copy(0, 1, q).start()
        z_copy(1, 1, q).start()
        items.append((q, z, q))
        launch(items[-1], 0)
        if q == 0:
            for k in range(1, NZ):
                lk_copy(k).start()

    for row in range(G // 32):
        parts = [edge[k:k + 1, row * 32:(row + 1) * 32] for k in range(K)]
        order[row:row + 1, :] = jnp.concatenate(parts + [jnp.zeros((1, 32), jnp.int32)], axis=1)
    load_slots = pltpu.make_async_copy(order, slots, pre.at[7])
    load_slots.start()

    loads[0].wait()
    loads[1].wait()
    landed = [items[0:2], items[2:4]]
    step = 0
    for d in range(1, 5):
        below, above = lax.rem(z + NZ - d, NZ), lax.rem(z + d, NZ)
        shards = (below, above) if d < 4 else (below,)
        for q in range(Q):
            for direction in range(2):
                if goes(direction, d, q):
                    z_copy(direction, d, q, arriving=True).wait_recv()
                    if d < 4 and goes(direction, d + 1, q):
                        z_copy(direction, d + 1, q).start()
            if q == 0:
                for i, shard in enumerate(shards):
                    lk_arrival(shard).wait_recv()
                    choose(shard, 1 + i)
            new = []
            for i, shard in enumerate(shards):
                items.append((q, shard, len(items)))
                new.append(items[-1])
                launch(items[-1], 1 + i)
            landed.append(new)
            if step < G // 128:
                grid_side(step)
            if step == G // 128:
                load_node.start()
            if len(landed) > 3:
                for item in landed.pop(0):
                    unpack(item)
            step += 1
    for group in landed:
        for item in group:
            unpack(item)

    loads[2].wait()
    loads[3].wait()
    loads[4].wait()
    load_node.wait()
    load_slots.wait()

    def m_copy(i, b, arriving=False):
        if b == NB - 1:
            whose = m
            to = [up, down, partner, far, up + other, down + other, far + other][i]
        else:
            whose, to = [
                (m, up), (m, down), (m, partner),
                (m, far) if b >= NB - 3 else (down, up) if b % 2 == 0 else (up, down),
                (down, partner), (up, partner), (far, partner),
            ][i]
        if arriving:
            whose = [down, up, partner, far, down + other, up + other, far + other][i]
        spot = X.at[whose, :, pl.ds(*BLOCKS[b])]
        return remote(spot, spot, m_s.at[b * 7 + i], m_r.at[b * 7 + i], member=to)

    def pass_on(b):
        first, second = (0, 1) if b % 2 == 0 else (1, 0)
        m_copy(first, b, True).wait_recv()
        if b < NB - 3:
            m_copy(3, b).start()
        m_copy(4 + first, b).start()
        m_copy(second, b, True).wait_recv()
        m_copy(4 + second, b).start()

    def pass_far(b):
        m_copy(3, b, True).wait_recv()
        m_copy(6, b).start()

    gain_row = gain[...]

    limit = rp[0]
    save_fields = pltpu.make_async_copy(fields_all, fields_out, pre.at[6])

    for b in range(NB):
        start, size = BLOCKS[b]

        @pl.loop(0, size // 32)
        def _(q):
            for u in range(32):
                p = start + q * 32 + u
                g = gs[pl.ds(pl.multiple_of(p * 8, 8), 8), :]
                total = jnp.zeros((8, 128), jnp.float32)
                for k in range(K):
                    half = F[slots[start // 32 + q, k * 32 + u]] + g
                    total = total + (half + half * jnp.tanh(half))
                S[pl.ds(q * 256 + (u // 8) * 64 + u % 8, 8, stride=8), :] = total

        cube = S[0:size * 8, :].reshape(size // 8, 8, 8, 128)
        summed = jnp.concatenate([cube[:, j].reshape(size, 128) for j in range(8)], axis=1)
        scale = lax.rsqrt(jnp.mean(summed * summed, axis=-1, keepdims=True) + EPSILON)
        normed = (summed * scale * gain_row).astype(jnp.bfloat16)
        half = 0.5 * jnp.dot(normed, square[...], preferred_element_type=jnp.float32)
        hidden = (half + half * jnp.tanh(half)).astype(jnp.bfloat16)
        fields = lax.dot_general(
            w_out[...], hidden, (((1,), (1,)), ((), ())), preferred_element_type=jnp.float32
        )
        point = lax.broadcasted_iota(jnp.int32, (C, size), 1) + start
        fields = jnp.where(point < limit, fields, 0.0).astype(jnp.bfloat16)
        X[m, 0:C, start:start + size] = fields
        X[m, C:CP, start:start + size] = jnp.zeros((CP - C, size), jnp.bfloat16)
        for i in range(7 if b == NB - 1 else 4 if b >= NB - 3 else 3):
            m_copy(i, b).start()
        fields_all[:, start:start + size] = fields
        if b == NB - 1:
            save_fields.start()
        if b >= 2:
            pass_on(b - 2)
        if b >= 4:
            pass_far(b - 4)

    def slope(v):
        return v * lax.rsqrt(v * v + SOFT_SCALE * SOFT_SCALE)

    line = jnp.concatenate([weight[...], jnp.zeros((1, 128 - C), jnp.float32)], axis=1)
    wide = jnp.transpose(jnp.broadcast_to(line, (128, 128)))[0:C, :]

    def score(b):
        start, size = BLOCKS[b]
        for i in (range(7) if b == NB - 1 else (2, 4, 5, 6)):
            m_copy(i, b, True).wait_recv()

        @pl.loop(0, size // 128)
        def _(t):
            tile = start // 128 + t
            lanes = pl.ds(pl.multiple_of(tile * 128, 128), 128)
            here = X[m, 0:C, lanes].astype(jnp.float32)
            pair = jnp.zeros((C, 128), jnp.float32)
            for k in range(1, MEMBERS):
                pair = pair + slope(here - X[lax.rem(m + k, MEMBERS), 0:C, lanes].astype(jnp.float32))
            total = slope(here - targets[:, lanes]) - pair * (1.0 / (MEMBERS - 1))
            point = lax.broadcasted_iota(jnp.int32, (C, 128), 1) + tile * 128
            score_out[pl.ds(tile, C, stride=G // 128), :] = jnp.where(point < limit, wide * total, 0.0)

    pass_far(NB - 4)
    for item in items[-SLOTS:]:
        for i in range(NX - 1):
            x_copy(i, item).wait_send()
    for d in range(1, 5):
        for q in range(Q):
            for direction in range(2):
                if goes(direction, d, q):
                    z_copy(direction, d, q).wait_send()
    for k in range(1, NZ):
        lk_copy(k).wait_send()
    score(0)
    pass_far(NB - 3)
    pass_on(NB - 2)
    score(1)
    score(2)
    pass_far(NB - 2)
    for b in range(3, NB):
        if b == NB - 1:
            for done in range(NB - 2):
                for i in range(7):
                    m_copy(i, done).wait_send()
        score(b)

    for b in range(NB - 2, NB):
        for i in range(7):
            m_copy(i, b).wait_send()
    save_fields.wait()


def decoder_call(edge, look, gain, weight, *arrays):
    n_items = Q * NZ
    vm = pl.BlockSpec(memory_space=pltpu.VMEM)
    hbm = pl.BlockSpec(memory_space=pltpu.HBM)
    dma = pltpu.SemaphoreType.DMA
    half, full = jnp.bfloat16, jnp.float32
    return pl.pallas_call(
        decoder_kernel,
        out_shape=(
            jax.ShapeDtypeStruct((C, G), half),
            jax.ShapeDtypeStruct((C * (G // 128), 128), full),
        ),
        in_specs=[vm, vm, vm, vm] + [hbm] * len(arrays),
        out_specs=(hbm, vm),
        scratch_shapes=[
            pltpu.VMEM((Q, NZ, NODES, W), half),
            pltpu.VMEM((SLOTS, NX - 1, CAP, W), half),
            pltpu.VMEM((n_items, NX - 1, CAP, W), half),
            pltpu.VMEM((NZ, NX, CAP), jnp.int32),
            pltpu.VMEM((3, NX * CAP, NODES), half),
            pltpu.VMEM((ROWS * CAP, 8, 128), full),
            pltpu.VMEM((G * 8, 128), full),
            pltpu.VMEM((PB * 8, 128), full),
            pltpu.VMEM((MEMBERS, CP, G), half),
            pltpu.VMEM((C, G), half),
            pltpu.VMEM((G // 32, 128), jnp.int32),
            pltpu.SMEM((G // 32, 128), jnp.int32),
            pltpu.SMEM((1,), jnp.int32),
            pltpu.VMEM((NODES, D), half),
            pltpu.VMEM((Q, D, W), half),
            pltpu.VMEM((G, D), half),
            pltpu.VMEM((D, D), half),
            pltpu.VMEM((C, D), half),
            pltpu.VMEM((C, G), full),
            dma((NZ,)), dma((NZ,)),
            dma((8 * Q,)), dma((8 * Q,)),
            dma((n_items * 3,)), dma((n_items * 3,)),
            dma((NB * 7,)), dma((NB * 7,)),
            dma((8,)), dma((Q + 1,)),
        ],
        compiler_params=pltpu.CompilerParams(
            collective_id=0, has_side_effects=True, vmem_limit_bytes=VMEM_LIMIT
        ),
        cost_estimate=pl.CostEstimate(flops=14 * 10**9, bytes_accessed=20 * MIB, transcendentals=0),
        name="decoder",
    )(edge, look, gain, weight, *arrays)


def place_kernel(a, b, a_out, b_out, sems):
    copies = [
        pltpu.make_async_copy(a, a_out, sems.at[0]),
        pltpu.make_async_copy(b, b_out, sems.at[1]),
    ]
    for copy in copies:
        copy.start()
    for copy in copies:
        copy.wait()


def place_call(a, b):
    vm = pl.BlockSpec(memory_space=pltpu.VMEM)
    hbm = pl.BlockSpec(memory_space=pltpu.HBM)
    return pl.pallas_call(
        place_kernel,
        out_shape=(jax.ShapeDtypeStruct(a.shape, a.dtype), jax.ShapeDtypeStruct(b.shape, b.dtype)),
        in_specs=[vm, vm],
        out_specs=(hbm, hbm),
        scratch_shapes=[pltpu.SemaphoreType.DMA((2,))],
        name="place",
    )(a, b)


def local(
    processed_latent_nodes, grid_embed, dispatch_node_lookup, send_count, edge_slot, row_points,
    w_src, w_dst, gain_node, w_node, w_out, targets, channel_weight,
):
    del send_count
    fields, score = decoder_call(
        edge_slot, dispatch_node_lookup.reshape(NZ, NX, CAP),
        gain_node[None, :], channel_weight[None, :],
        row_points, processed_latent_nodes[0], w_src, grid_embed, w_dst, w_node, w_out, targets,
    )
    fields, score = place_call(fields, score)
    return fields[None], score.reshape(1, C, G)


def solution(mesh):
    placed = (
        P("member", "rows", None),
        P("rows", None),
        P("rows", None),
        P("rows"),
        P(None, "rows"),
        P("rows"),
        P(),
        P(),
        P(),
        P(),
        P(),
        P(None, "rows"),
        P(),
    )
    return jax.shard_map(
        local,
        mesh=mesh,
        in_specs=placed,
        out_specs=(P("member", None, "rows"), P("member", None, "rows")),
        check_vma=False,
    )
```
